32 devices in a mesh: dom: 2 (over x), space: 16 (over z, y, core).
Axes of the slice: x: 2, y: 2, z: 4, core: 2. Of those that a mesh axis runs over, the one named last changes fastest.
Arguments:
- inputs: bfloat16 [2, 32, 2048, 2048], P('dom', None, 'space'), parts along dimension 0, may hold values from -10.5 to 10.5
- target: bfloat16 [2, 32, 2048, 2048], P('dom', None, 'space'), parts along dimension 0, may hold values from -6 to 6
- spectral_weight: float32 [64, 32, 32, 128], P('space'), may hold values from -18 to 18
- local_weight: bfloat16 [32, 32], replicated, may hold values from -1 to 1
- bias_term: float32 [32], replicated, may hold values from -3 to 3
Outputs:
- grad_input: bfloat16 [2, 32, 2048, 2048], P('dom', None, 'space'), parts along dimension 0
- grad_spectral: float32 [64, 64, 32, 128], P('space', 'dom'), parts along dimension 1
- grad_local: float32 [64, 32], P('dom'), parts along dimension 0
- grad_bias: float32 [64], P('dom'), parts along dimension 0
The draws below stay inside these ranges and needn't reach their ends.
There are 2 independent parts, one for each index of `dom`. The reference program is written for one: setup_inputs(seed, part) draws one part's arguments, and reference() takes and returns one part's arrays. A program takes and returns all parts, laid end to end along the dimension named above; an argument that names none is the same for every part. Nothing has to cross between parts.
All inputs are finite; a program needn't handle non-finite values.
Results may differ from the reference program's by a relative error of at most 0.014.
Values may be sent and summed in bfloat16 or wider, within the bound.
A program may use at most 192 MiB of HBM per device.

```python
import math
import jax
import jax.numpy as jnp
from jax import lax

C = 32
H = 2048
W = 2048
KX = 64
KY = 64
STEPS = 1


def draw_inputs(key, part):
    row_place = jnp.arange(H, dtype=jnp.float32) / (H - 1) - 0.5
    noise_field = jax.random.truncated_normal(key, -6.0, 6.0, (STEPS, C, H, W), jnp.float32)
    factor = jnp.power(3.0, row_place)
    return (noise_field * factor[None, None, :, None]).astype(jnp.bfloat16)


def levels(rng, extent, pieces, low, high):
    gain = 1.0
    for dim, parts in pieces:
        heights = jax.random.uniform(jax.random.fold_in(jax.random.fold_in(rng, 6), dim), (parts,), jnp.float32, low / len(pieces), high / len(pieces))
        gain = gain * jnp.repeat(jnp.exp(heights), extent[dim] // parts).reshape((-1,) + (1,) * (len(extent) - 1 - dim))
    return gain


def centred(key, dims, width, bound, cuts=(), held_as=jnp.bfloat16):
    entries = jax.random.normal(key, dims, jnp.float32) * width
    if len(cuts) > 0:
        entries = levels(key, dims, cuts, -0.22, 0.18) * entries
    return jnp.clip(entries, min=-bound, max=bound).astype(held_as)


def setup_inputs(seed: int = 0, part: int = 0) -> dict:
    seeds = jax.random.split(jax.random.key(seed), 6)
    part_splits = jax.random.split(jax.random.fold_in(seeds[5], part), 6)
    inputs = draw_inputs(jax.random.fold_in(jax.random.fold_in(seeds[5], part), 71), part)
    target = centred(part_splits[1], (STEPS, C, H, W), 1.0, 6.0, ((2, 16),))
    spectral_weight = centred(seeds[2], (KY, C, C, 2 * KX), 3.0, 18.0, ((0, 16),), jnp.float32)
    local_weight = centred(seeds[3], (C, C), C ** -0.5, 1.0)
    bias_term = centred(seeds[4], (C,), 1.0, 3.0, (), jnp.float32)
    return dict(inputs=inputs, target=target, spectral_weight=spectral_weight, local_weight=local_weight, bias_term=bias_term)


PRECISE = lax.Precision.HIGHEST

def row_table():
    mode_index = jnp.arange(KY, dtype=jnp.int32)[:, None]
    column = jnp.arange(W, dtype=jnp.int32)[None, :]
    angles = (mode_index * column % W).astype(jnp.float32) * (2.0 * math.pi / W)
    factor = 1.0 / math.sqrt(H * W)
    return jnp.stack([jnp.cos(angles) * factor, -jnp.sin(angles) * factor]).astype(jnp.bfloat16)

def column_table(row_index):
    column = jnp.arange(KX, dtype=jnp.int32)
    frequency = jnp.where(column < KX // 2, column, column + H - KX)
    angles = (row_index[:, None] * frequency[None, :] % H).astype(jnp.float32) * (2.0 * math.pi / H)
    return jnp.concatenate([jnp.cos(angles), jnp.sin(angles)], axis=1)

def mode_weights(start_mode, mode_count):
    mode_index = start_mode + jnp.arange(mode_count, dtype=jnp.int32)
    return jnp.where(mode_index == 0, 1.0, 2.0).astype(jnp.float32)

def row_analysis(field_data, basis):
    return jnp.einsum('schw,pkw->kpsch', field_data.astype(jnp.float32), basis.astype(jnp.float32))

def row_synth(spectra, basis):
    return jnp.einsum('kpsch,pkw->schw', spectra.astype(jnp.float32), basis.astype(jnp.float32))

def column_modes(slab_part, basis):
    product = jnp.einsum('kpsch,hj->kpscj', slab_part, basis, precision=PRECISE)
    half_count = basis.shape[1] // 2
    real_part = product[:, 0, :, :, :half_count] + product[:, 1, :, :, half_count:]
    imag_part = product[:, 1, :, :, :half_count] - product[:, 0, :, :, half_count:]
    return jnp.concatenate([real_part, imag_part], axis=-1)

def column_synth(mode_data, basis):
    half_count = basis.shape[1] // 2
    real_part, imag_part = (mode_data[..., :half_count], mode_data[..., half_count:])
    cosines, sine_part = (basis[:, :half_count], basis[:, half_count:])
    first_part = jnp.einsum('ysok,hk->ysoh', real_part, cosines, precision=PRECISE) - jnp.einsum('ysok,hk->ysoh', imag_part, sine_part, precision=PRECISE)
    second = jnp.einsum('ysok,hk->ysoh', real_part, sine_part, precision=PRECISE) + jnp.einsum('ysok,hk->ysoh', imag_part, cosines, precision=PRECISE)
    return jnp.stack([first_part, second], axis=1).astype(jnp.bfloat16)

def split_complex(mode_data):
    half_count = mode_data.shape[-1] // 2
    return (mode_data[..., :half_count], mode_data[..., half_count:])

def mix_modes(input_modes, weight):
    spec_real, spec_imag = split_complex(input_modes)
    weight_real, weight_imag = split_complex(weight)
    form = 'ysck,ycok->ysok'
    out_real = jnp.einsum(form, spec_real, weight_real, precision=PRECISE) - jnp.einsum(form, spec_imag, weight_imag, precision=PRECISE)
    out_imag = jnp.einsum(form, spec_real, weight_imag, precision=PRECISE) + jnp.einsum(form, spec_imag, weight_real, precision=PRECISE)
    return jnp.concatenate([out_real, out_imag], axis=-1)

def mix_back(delta_modes, weight):
    delta_real, delta_imag = split_complex(delta_modes)
    weight_real, weight_imag = split_complex(weight)
    form = 'ysok,ycok->ysck'
    out_real = jnp.einsum(form, delta_real, weight_real, precision=PRECISE) + jnp.einsum(form, delta_imag, weight_imag, precision=PRECISE)
    out_imag = jnp.einsum(form, delta_imag, weight_real, precision=PRECISE) - jnp.einsum(form, delta_real, weight_imag, precision=PRECISE)
    return jnp.concatenate([out_real, out_imag], axis=-1)

def mix_grad(input_modes, delta_modes):
    spec_real, spec_imag = split_complex(input_modes)
    delta_real, delta_imag = split_complex(delta_modes)
    form = 'ysck,ysok->ycok'
    grad_real = jnp.einsum(form, spec_real, delta_real, precision=PRECISE) + jnp.einsum(form, spec_imag, delta_imag, precision=PRECISE)
    grad_imag = jnp.einsum(form, spec_real, delta_imag, precision=PRECISE) - jnp.einsum(form, spec_imag, delta_real, precision=PRECISE)
    return jnp.concatenate([grad_real, grad_imag], axis=-1)

def gelu_parts(value):
    normal_cdf = 0.5 * (1.0 + jax.scipy.special.erf(value * (1.0 / math.sqrt(2.0))))
    density = jnp.exp(-0.5 * value * value) * (1.0 / math.sqrt(2.0 * math.pi))
    return (value * normal_cdf, normal_cdf + value * density)

def reference(inputs, target, spectral_weight, local_weight, bias_term):
    row_basis = row_table()
    column_basis = column_table(jnp.arange(H, dtype=jnp.int32))
    mode_gain = mode_weights(0, KY)[:, None, None, None]
    input_modes = column_modes(row_analysis(inputs, row_basis), column_basis)
    mixed_modes = mix_modes(input_modes, spectral_weight) * mode_gain
    local_term = jnp.einsum('co,schw->sohw', local_weight.astype(jnp.float32), inputs.astype(jnp.float32))
    preact = row_synth(column_synth(mixed_modes, column_basis), row_basis) + local_term + bias_term[None, :, None, None]
    activated, derivative = gelu_parts(preact)
    delta_pre = ((activated - target.astype(jnp.float32)) * derivative).astype(jnp.bfloat16)
    delta_modes = column_modes(row_analysis(delta_pre, row_basis), column_basis) * mode_gain
    grad_spectral = mix_grad(input_modes, delta_modes)
    back_modes = mix_back(delta_modes, spectral_weight)
    back_local = jnp.einsum('co,sohw->schw', local_weight.astype(jnp.float32), delta_pre.astype(jnp.float32))
    grad_input = (row_synth(column_synth(back_modes, column_basis), row_basis) + back_local).astype(jnp.bfloat16)
    cell_count = STEPS * H * W
    grad_local = jnp.einsum('schw,sohw->co', inputs.astype(jnp.float32), delta_pre.astype(jnp.float32)) / cell_count
    grad_bias = lax.optimization_barrier(jnp.sum(delta_pre.astype(jnp.float32), axis=(0, 2, 3))) / cell_count
    return (grad_input, grad_spectral, grad_local, grad_bias)
```

```python
import functools
import math

import jax
import jax.numpy as jnp
import ml_dtypes
import numpy as np
from jax import lax
from jax.experimental import pallas as pl
from jax.experimental.pallas import tpu as pltpu
from jax.sharding import PartitionSpec as P

KX = 64
KY = 64
LANES = 2 * KX
QUARTER = KY // 4
LIMIT = 56 * 1024 * 1024
ROWS = 16
F32 = jnp.float32
BF16 = jnp.bfloat16
NT = (((1,), (1,)), ((), ()))
dot = functools.partial(jnp.dot, preferred_element_type=F32)
dot_nt = functools.partial(lax.dot_general, dimension_numbers=NT, preferred_element_type=F32)


def mode_order(devices):
    own = KY // devices
    return np.arange(KY).reshape(devices // 4, 2, 2, own).transpose(2, 1, 0, 3).reshape(-1)


def row_table(height, width, order):
    angles = (order[:, None] * np.arange(width)[None, :] % width) * (2.0 * math.pi / width)
    factor = 1.0 / math.sqrt(height * width)
    return np.concatenate([np.cos(angles) * factor, -np.sin(angles) * factor]).astype(ml_dtypes.bfloat16)


def column_table(height, devices):
    column = np.arange(KX)
    frequency = np.where(column < KX // 2, column, column + height - KX)
    angles = (np.arange(height)[:, None] * frequency[None, :] % height) * (2.0 * math.pi / height)
    cosines, sines = np.cos(angles), np.sin(angles)
    parts = np.stack([np.concatenate([cosines, -sines], 1), np.concatenate([sines, cosines], 1)])
    slab = height // devices
    table = parts.reshape(2, devices, slab, LANES).transpose(1, 0, 2, 3).reshape(devices, 2 * slab, LANES)
    table = table.astype(np.float32)
    hi = table.astype(ml_dtypes.bfloat16)
    lo = (table - hi.astype(np.float32)).astype(ml_dtypes.bfloat16)
    return np.concatenate([hi, lo], axis=2)


def halves(value):
    half = value.shape[-1] // 2
    return value[..., :half], value[..., half:]


def cat(a, b):
    return jnp.concatenate([a, b], axis=-1)


def columns_of(row_modes, table):
    parts = []
    for value in row_modes:
        turned = value.T
        parts.append(cat(turned[:KY], turned[KY:]))
    both = jnp.concatenate(parts, axis=0).astype(BF16)
    hi, lo = halves(dot(both, table))
    return hi + lo


def expand_rows(z_ref, table, slab, e_ref):
    chans = z_ref.shape[2]
    left = table[:slab]
    pair = 2

    def body(i, carry):
        parts = []
        for k in range(pair):
            z = z_ref[:, :, i * pair + k].reshape(KY, LANES)
            re, im = halves(z)
            both = jnp.concatenate([z, cat(im, -re)], axis=0)
            parts.append(cat(both, both))
        out = dot_nt(left, jnp.concatenate(parts, axis=0)).astype(BF16)
        for k in range(pair):
            e_ref[i * pair + k] = out[:, k * 2 * KY : (k + 1) * 2 * KY]
        return carry

    lax.fori_loop(0, chans // pair, body, 0)


def place():
    devices = lax.axis_size("space")
    me = lax.axis_index("space")
    return devices // 4, me, lax.rem(me, 2), lax.rem(me // 2, 2), me // 4


def peers():
    nz, me, core, mid, z = place()
    across = me + 1 - 2 * core
    beside = me + 2 - 4 * mid
    along = [lax.rem(z + i, nz) for i in range(nz)]
    return across, beside, along, [a * 4 + mid * 2 + core for a in along]


def greet():
    across, beside, _, line = peers()
    barrier = pltpu.get_barrier_semaphore()
    for target in [across, beside] + line[1:]:
        pl.semaphore_signal(barrier, inc=1, device_id={"space": target}, device_id_type=pl.DeviceIdType.MESH)


def greeted():
    pl.semaphore_wait(pltpu.get_barrier_semaphore(), len(peers()[3]) + 1)


class Links:
    def __init__(self, send_sem, recv_sem):
        self.send_sem, self.recv_sem, self.used, self.copies = send_sem, recv_sem, 0, []

    def start(self, src, dst, target):
        copy = pltpu.make_async_remote_copy(
            src_ref=src,
            dst_ref=dst,
            send_sem=self.send_sem.at[self.used],
            recv_sem=self.recv_sem.at[self.used],
            device_id={"space": target},
            device_id_type=pl.DeviceIdType.MESH,
        )
        copy.start()
        self.used += 1
        self.copies.append(copy)
        return copy

    def finish(self):
        for copy in self.copies:
            copy.wait_send()


def exchange_scratch(devices, chans, own, small):
    nz = devices // 4
    count = 5 + 2 * (nz - 1) + (nz + 1 if small else 0)
    shapes = [
        pltpu.VMEM((2, 2, chans, QUARTER, LANES), BF16),
        pltpu.VMEM((2, chans, QUARTER, LANES), BF16),
        pltpu.VMEM((chans, QUARTER, LANES), BF16),
        pltpu.VMEM((chans, QUARTER, LANES), BF16),
        pltpu.VMEM((chans, QUARTER, LANES), F32),
        pltpu.VMEM((nz, own, chans, LANES), F32),
        pltpu.VMEM((nz, own, chans, LANES), BF16),
        pltpu.VMEM((nz, own, chans, LANES), BF16),
        pltpu.VMEM((nz, own, chans, LANES), BF16),
        pltpu.VMEM((2, 2, chans, QUARTER, LANES), BF16),
        pltpu.VMEM((own, chans, chans, LANES), F32),
        pltpu.SemaphoreType.DMA((count,)),
        pltpu.SemaphoreType.DMA((count,)),
        pltpu.SemaphoreType.DMA,
        pltpu.SemaphoreType.DMA,
    ]
    if small:
        shapes += [pltpu.VMEM((4, chans, LANES), F32), pltpu.VMEM((nz, chans, LANES), F32)]
    return shapes


def exchange(scratch, mix, own_ref, z_ref, small_ref=None):
    m, r1, s2, r2, acc, s3f, s3, r3, zg, zt = scratch[:10]
    nz, me, core, mid, z = place()
    across, beside, along, line = peers()
    chans = m.shape[2]
    own = s3.shape[1]
    links = Links(scratch[11], scratch[12])

    first = links.start(m.at[1 - core], r1, across)
    if small_ref is not None:
        sm, rz = scratch[15:17]
        small_first = links.start(sm.at[0], sm.at[1], across)
    first.wait_recv()
    s2[...] = (m[core, 1 - mid].astype(F32) + r1[1 - mid].astype(F32)).astype(BF16)
    second = links.start(s2, r2, beside)
    if small_ref is not None:
        small_first.wait_recv()
        sm[2] = sm[0] + sm[1]
        small_second = links.start(sm.at[2], sm.at[3], beside)
    acc[...] = m[core, mid].astype(F32) + r1[mid].astype(F32)
    second.wait_recv()
    acc[...] += r2[...].astype(F32)
    for a in range(nz):
        for k in range(own):
            block = acc[:, a * own + k, :]
            s3f[a, k] = block
            s3[a, k] = block.astype(BF16)
    sums = [links.start(s3.at[along[i]], r3.at[i], line[i]) for i in range(1, nz)]
    if small_ref is not None:
        small_second.wait_recv()
        rz[z] = sm[2] + sm[3]
        smalls = [links.start(rz.at[z], rz.at[z], line[i]) for i in range(1, nz)]
    for i in range(1, nz):
        sums[i - 1].wait_recv()
    for k in range(own):
        total = s3f[z, k]
        for i in range(1, nz):
            total = total + r3[i, k].astype(F32)
        own_ref[k] = total

    mix(own_ref, zg, z)
    gathered = [links.start(zg.at[z], zg.at[z], line[i]) for i in range(1, nz)]
    if small_ref is not None:
        for copy in smalls:
            copy.wait_recv()
        total = rz[0]
        for i in range(1, nz):
            total = total + rz[i]
        small_ref[...] = total
    for copy in gathered:
        copy.wait_recv()
    for a in range(nz):
        for k in range(own):
            acc[:, a * own + k, :] = zg[a, k].astype(F32)
    zt[core, mid] = acc[...].astype(BF16)
    side = links.start(zt.at[core, mid], zt.at[core, mid], beside)
    near = links.start(zt.at[core, mid], zt.at[core, mid], across)
    side.wait_recv()
    far = links.start(zt.at[core, 1 - mid], zt.at[core, 1 - mid], across)
    near.wait_recv()
    far.wait_recv()
    links.finish()
    z_ref[...] = zt[...]


def mode_gain(me, own, k):
    return jnp.where(me * own + k == 0, 1.0, 2.0).astype(F32)


def swap(value):
    a, b = halves(value)
    return cat(b, a)


def mix_forward(w_ref, me, x_ref, z_ref, z):
    own, chans = w_ref.shape[:2]
    for k in range(own):
        x = x_ref[k]
        x_sw = swap(x)
        first = jnp.zeros(w_ref.shape[2:], F32)
        second = jnp.zeros(w_ref.shape[2:], F32)
        for c in range(chans):
            w = w_ref[k, c]
            first = first + x[c : c + 1] * w
            second = second + x_sw[c : c + 1] * w
        a, b = halves(first)
        c, d = halves(second)
        z_ref[z, k] = (cat(a - b, c + d) * mode_gain(me, own, k)).astype(BF16)


def mix_back(w_ref, me, d_ref, z_ref, z):
    own, chans = w_ref.shape[:2]
    for k in range(own):
        d = d_ref[k] * mode_gain(me, own, k)
        d_ref[k] = d
        d_sw = swap(d)
        firsts, seconds = [], []
        for c in range(chans):
            w = w_ref[k, c]
            firsts.append(jnp.sum(d * w, axis=0, keepdims=True))
            seconds.append(jnp.sum(d_sw * w, axis=0, keepdims=True))
        a, b = halves(jnp.concatenate(firsts, axis=0))
        e, f = halves(jnp.concatenate(seconds, axis=0))
        z_ref[z, k] = cat(a + b, e - f).astype(BF16)


def analysis_kernel(x_ref, bt_ref, cols_ref, w_ref, z_ref, own_ref, cols, *scratch):
    step = pl.program_id(0)
    count, rows, width = x_ref.shape
    m, wv, w_sem, c_sem = scratch[0], scratch[10], scratch[13], scratch[14]
    me = lax.axis_index("space")
    weights = pltpu.make_async_copy(w_ref, wv, w_sem)
    table = pltpu.make_async_copy(cols_ref.at[me], cols, c_sem)

    @pl.when(step == 0)
    def _():
        greet()
        table.start()
        weights.start()
        table.wait()

    flat = x_ref[...].reshape(count * rows, width)
    row_modes = dot(flat, bt_ref[...])
    modes = columns_of([row_modes[c * rows : (c + 1) * rows] for c in range(count)], cols[...]).astype(BF16)
    for c in range(count):
        m[:, :, step * count + c] = modes[c * KY : (c + 1) * KY].reshape(2, 2, QUARTER, LANES)

    @pl.when(step == pl.num_programs(0) - 1)
    def _():
        greeted()
        weights.wait()
        exchange(scratch, functools.partial(mix_forward, wv, me), own_ref, z_ref)


def whole(a):
    return pl.BlockSpec(a.shape, lambda i: (0,) * a.ndim)


def held(shape):
    return pl.BlockSpec(shape, lambda i: (0,) * len(shape))


HBM = pl.BlockSpec(memory_space=pl.ANY)


def analysis(x, bt, cols, weight, devices):
    chans, rows, width = x.shape
    own = weight.shape[0]
    block = 4
    shapes = [
        jax.ShapeDtypeStruct((2, 2, chans, QUARTER, LANES), BF16),
        jax.ShapeDtypeStruct((own, chans, LANES), F32),
    ]
    return pl.pallas_call(
        analysis_kernel,
        grid=(chans // block,),
        in_specs=[pl.BlockSpec((block, rows, width), lambda i: (i, 0, 0)), whole(bt), HBM, HBM],
        out_specs=[held(s.shape) for s in shapes],
        out_shape=shapes,
        scratch_shapes=[pltpu.VMEM(cols.shape[1:], BF16)] + exchange_scratch(devices, chans, own, False),
        compiler_params=pltpu.CompilerParams(vmem_limit_bytes=LIMIT, collective_id=0, has_side_effects=True),
        name="analysis",
    )(x, bt, cols, weight)


def spread(weight, flip, scale):
    chans = weight.shape[0]
    flat = chans * ROWS
    chosen = lax.broadcasted_iota(jnp.int32, (flat, chans), 0) // ROWS == lax.broadcasted_iota(jnp.int32, (flat, chans), 1)
    chosen = jnp.where(chosen, 1.0, 0.0).astype(BF16)
    tall = (dot_nt if flip else dot)(chosen, weight).astype(BF16)
    wide = dot_nt(tall, chosen)
    first = lax.broadcasted_iota(jnp.int32, (flat, flat), 0) % ROWS
    second = lax.broadcasted_iota(jnp.int32, (flat, flat), 1) % ROWS
    return jnp.where(first == second, wide * scale, 0.0).astype(BF16)


PHI = (1.5954356609777183, 0.29438608777535386, -0.010105857224310238)


def twice_delta(s, target):
    q = s * s
    p = jnp.minimum(q, 9.0)
    p = (PHI[2] * p + PHI[1]) * p + PHI[0]
    a = 1.0 + jnp.tanh(s * p)
    e = jnp.exp2(q * (-2.0 / math.log(2.0)) + math.log2(4.0 / math.sqrt(2.0 * math.pi)))
    return (s * a - target) * (a + s * e)


def forward_kernel(x_ref, t_ref, z_ref, lw_ref, bias_ref, rb_ref, bt_ref, cols_ref, w_ref,
                   delta_ref, back_ref, dm_ref, small_ref, cols, kron, rows_ref, acc_ref, e_ref, *scratch):
    step = pl.program_id(0)
    chans, rows, width = x_ref.shape
    slab = rows_ref.shape[1]
    flat = chans * rows
    tile = 512
    m, wv, w_sem, c_sem = scratch[0], scratch[10], scratch[13], scratch[14]
    sm = scratch[15]
    me = lax.axis_index("space")
    weights = pltpu.make_async_copy(w_ref, wv, w_sem)
    table = pltpu.make_async_copy(cols_ref.at[me], cols, c_sem)

    @pl.when(step == 0)
    def _():
        greet()
        table.start()
        weights.start()
        acc_ref[...] = jnp.zeros_like(acc_ref)
        kron[...] = spread(lw_ref[...], True, 0.5)
        table.wait()
        expand_rows(z_ref, cols[...], slab, e_ref)

    band = pl.ds(pl.multiple_of(step * rows, rows), rows)
    e = (e_ref[:, band, :].reshape(flat, LANES).astype(F32) * 0.5).astype(BF16)
    row_modes = jnp.zeros((flat, bt_ref.shape[1]), F32)
    bias = jnp.broadcast_to((bias_ref[...] * 0.5)[:, None, :], (chans, rows, LANES)).reshape(flat, LANES)[:, :1]
    for start in range(0, width, tile):
        cells = pl.ds(start, tile)
        x = x_ref[:, :, cells].reshape(flat, tile)
        s = dot(e, rb_ref[:, cells]) + dot(kron[...], x) + bias
        target = t_ref[:, :, cells].reshape(flat, tile).astype(F32)
        delta = twice_delta(s, target).astype(BF16)
        delta_ref[:, :, cells] = delta.reshape(chans, rows, tile)
        row_modes = row_modes + dot(delta, bt_ref[cells, :])
        acc_ref[...] += dot_nt(x, delta)
    rows_ref[:, band, :] = (row_modes * 0.5).reshape(chans, rows, -1)

    @pl.when(step == pl.num_programs(0) - 1)
    def _():
        count = 4

        def body(i, carry):
            modes = columns_of([rows_ref[i * count + k] for k in range(count)], cols[...]).astype(BF16)
            for k in range(count):
                m[:, :, i * count + k] = modes[k * KY : (k + 1) * KY].reshape(2, 2, QUARTER, LANES)
            return carry

        lax.fori_loop(0, chans // count, body, 0)
        first = lax.broadcasted_iota(jnp.int32, (flat, flat), 0) % rows
        second = lax.broadcasted_iota(jnp.int32, (flat, flat), 1) % rows
        kept = jnp.where(first == second, acc_ref[...], 0.0)
        kept = jnp.sum(kept.reshape(chans, rows, flat), axis=1)
        group = lax.broadcasted_iota(jnp.int32, (flat, LANES), 0) // rows
        lane = lax.broadcasted_iota(jnp.int32, (flat, LANES), 1)
        group = jnp.where(group == lane, 0.5, 0.0).astype(BF16)
        hi = kept.astype(BF16)
        rest = kept - hi.astype(F32)
        lo = rest.astype(BF16)
        last = (rest - lo.astype(F32)).astype(BF16)
        terms = dot(hi, group) + (dot(lo, group) + dot(last, group))
        sums = jnp.sum(rows_ref[...], axis=1)[:, :1]
        lane = lax.broadcasted_iota(jnp.int32, (chans, LANES), 1)
        sm[0] = jnp.where(lane == chans, sums, terms)
        greeted()
        weights.wait()
        exchange(scratch, functools.partial(mix_back, wv, me), dm_ref, back_ref, small_ref)


def forward(x, target, z, local_weight, bias, rb, bt, cols, weight, devices):
    chans, slab, width = x.shape
    own = weight.shape[0]
    flat = chans * ROWS
    band = pl.BlockSpec((chans, ROWS, width), lambda i: (0, i, 0))
    shapes = [
        jax.ShapeDtypeStruct(x.shape, BF16),
        jax.ShapeDtypeStruct((2, 2, chans, QUARTER, LANES), BF16),
        jax.ShapeDtypeStruct((own, chans, LANES), F32),
        jax.ShapeDtypeStruct((chans, LANES), F32),
    ]
    return pl.pallas_call(
        forward_kernel,
        grid=(slab // ROWS,),
        in_specs=[band, band, whole(z), whole(local_weight), whole(bias), whole(rb), whole(bt), HBM, HBM],
        out_specs=[band] + [held(s.shape) for s in shapes[1:]],
        out_shape=shapes,
        scratch_shapes=[
            pltpu.VMEM(cols.shape[1:], BF16),
            pltpu.VMEM((flat, flat), BF16),
            pltpu.VMEM((chans, slab, 2 * KY), F32),
            pltpu.VMEM((flat, flat), F32),
            pltpu.VMEM((chans, slab, 2 * KY), BF16),
        ] + exchange_scratch(devices, chans, own, True),
        compiler_params=pltpu.CompilerParams(vmem_limit_bytes=LIMIT, collective_id=1, has_side_effects=True),
        name="forward",
    )(x, target, z, local_weight, bias, rb, bt, cols, weight)


def final_kernel(root, cells_count, d_ref, z_ref, lw_ref, rb_ref, cols_ref, xm_ref, dm_ref, small_ref,
                 out_ref, g_ref, local_ref, bias_ref, cols, kron, e_ref, c_sem):
    step = pl.program_id(0)
    chans, rows, width = d_ref.shape
    slab = e_ref.shape[1]
    flat = chans * rows
    tile = 512
    pairs = g_ref.shape[0]
    me = lax.axis_index("space")
    table = pltpu.make_async_copy(cols_ref.at[me], cols, c_sem)

    @pl.when(step == 0)
    def _():
        table.start()
        kron[...] = spread(lw_ref[...], False, 0.5)
        small = small_ref[...]
        local_ref[...] = small[:, :chans] * (1.0 / cells_count)
        column = small[:, chans : chans + 1] * (root / cells_count)
        eye = lax.broadcasted_iota(jnp.int32, (chans, chans), 0) == lax.broadcasted_iota(jnp.int32, (chans, chans), 1)
        bias_ref[...] = jnp.sum(jnp.where(eye, column, 0.0), axis=0, keepdims=True)
        table.wait()
        expand_rows(z_ref, cols[...], slab, e_ref)

    e = e_ref[:, pl.ds(pl.multiple_of(step * rows, rows), rows), :].reshape(flat, LANES)
    for start in range(0, width, tile):
        cells = pl.ds(start, tile)
        d = d_ref[:, :, cells].reshape(flat, tile)
        v = dot(e, rb_ref[:, cells]) + dot(kron[...], d)
        out_ref[:, :, cells] = v.astype(BF16).reshape(chans, rows, tile)
    for i in range(pairs):
        index = step * pairs + i
        x = xm_ref[pl.ds(index, 1), :]
        re, im = halves(x)
        d = dm_ref[index // chans]
        g_ref[i] = cat(re, re) * d + cat(im, -im) * swap(d)


def final(delta, z, local_weight, rb, cols, own_modes, delta_modes, small, height):
    chans, slab, width = delta.shape
    own = own_modes.shape[0]
    flat = chans * ROWS
    steps = slab // ROWS
    pairs = own * chans // steps
    band = pl.BlockSpec((chans, ROWS, width), lambda i: (0, i, 0))
    own_modes = own_modes.reshape(own * chans, LANES)
    cells_count = height * width
    return pl.pallas_call(
        functools.partial(final_kernel, math.sqrt(cells_count), cells_count),
        grid=(steps,),
        in_specs=[band, whole(z), whole(local_weight), whole(rb), HBM, whole(own_modes), whole(delta_modes), whole(small)],
        out_specs=[
            band,
            pl.BlockSpec((pairs, chans, LANES), lambda i: (i, 0, 0)),
            held((chans, chans)),
            held((1, chans)),
        ],
        out_shape=[
            jax.ShapeDtypeStruct(delta.shape, BF16),
            jax.ShapeDtypeStruct((own * chans, chans, LANES), F32),
            jax.ShapeDtypeStruct((chans, chans), F32),
            jax.ShapeDtypeStruct((1, chans), F32),
        ],
        scratch_shapes=[
            pltpu.VMEM(cols.shape[1:], BF16),
            pltpu.VMEM((flat, flat), BF16),
            pltpu.VMEM((chans, slab, 2 * KY), BF16),
            pltpu.SemaphoreType.DMA,
        ],
        compiler_params=pltpu.CompilerParams(vmem_limit_bytes=LIMIT),
        name="final",
    )(delta, z, local_weight, rb, cols, own_modes, delta_modes, small)


def per_device(inputs, target, spectral_weight, local_weight, bias_term):
    samples, chans, slab, width = inputs.shape
    devices = lax.axis_size("space")
    height = slab * devices

    table = row_table(height, width, mode_order(devices))
    rb = jnp.asarray(table)
    bt = jnp.asarray(np.ascontiguousarray(table.T))
    cols = jnp.asarray(column_table(height, devices))
    bias = jnp.broadcast_to(bias_term[:, None], (chans, LANES))

    x = inputs.reshape(chans, slab, width)
    z, own_modes = analysis(x, bt, cols, spectral_weight, devices)
    delta, z, delta_modes, small = forward(
        x, target.reshape(chans, slab, width), z, local_weight, bias, rb, bt, cols, spectral_weight, devices
    )
    grad_input, grad_spectral, grad_local, grad_bias = final(
        delta, z, local_weight, rb, cols, own_modes, delta_modes, small, height
    )
    return (
        grad_input.reshape(inputs.shape),
        grad_spectral.reshape(spectral_weight.shape),
        grad_local,
        grad_bias.reshape(chans),
    )


def solution(mesh):
    return jax.shard_map(
        per_device,
        mesh=mesh,
        in_specs=(
            P("dom", None, "space", None),
            P("dom", None, "space", None),
            P("space", None, None, None),
            P(),
            P(),
        ),
        out_specs=(
            P("dom", None, "space", None),
            P("space", "dom", None, None),
            P("dom", None),
            P("dom"),
        ),
        check_vma=False,
    )
```

```python
import functools
import math

import jax
import jax.numpy as jnp
import ml_dtypes
import numpy as np
from jax import lax
from jax.experimental import pallas as pl
from jax.experimental.pallas import tpu as pltpu
from jax.sharding import PartitionSpec as P

KX = 64
KY = 64
LANES = 2 * KX
QUARTER = KY // 4
LIMIT = 56 * 1024 * 1024
ROWS = 16
GROUP = 8
F32 = jnp.float32
BF16 = jnp.bfloat16
NT = (((1,), (1,)), ((), ()))
dot = functools.partial(jnp.dot, preferred_element_type=F32)
dot_nt = functools.partial(lax.dot_general, dimension_numbers=NT, preferred_element_type=F32)


def mode_order(devices):
    own = KY // devices
    return np.arange(KY).reshape(devices // 4, 2, 2, own).transpose(2, 1, 0, 3).reshape(-1)


def row_table(height, width, order):
    angles = (order[:, None] * np.arange(width)[None, :] % width) * (2.0 * math.pi / width)
    factor = 1.0 / math.sqrt(height * width)
    return np.concatenate([np.cos(angles) * factor, -np.sin(angles) * factor]).astype(ml_dtypes.bfloat16)


def column_table(height, devices):
    column = np.arange(KX)
    frequency = np.where(column < KX // 2, column, column + height - KX)
    angles = (np.arange(height)[:, None] * frequency[None, :] % height) * (2.0 * math.pi / height)
    cosines, sines = np.cos(angles), np.sin(angles)
    parts = np.stack([np.concatenate([cosines, -sines], 1), np.concatenate([sines, cosines], 1)])
    slab = height // devices
    table = parts.reshape(2, devices, slab, LANES).transpose(1, 0, 2, 3).reshape(devices, 2 * slab, LANES)
    table = table.astype(np.float32)
    hi = table.astype(ml_dtypes.bfloat16)
    lo = (table - hi.astype(np.float32)).astype(ml_dtypes.bfloat16)
    return np.concatenate([hi, lo], axis=2)


def halves(value):
    half = value.shape[-1] // 2
    return value[..., :half], value[..., half:]


def cat(a, b):
    return jnp.concatenate([a, b], axis=-1)


def columns_of(row_modes, table):
    parts = []
    for value in row_modes:
        turned = value.T
        parts.append(cat(turned[:KY], turned[KY:]))
    both = jnp.concatenate(parts, axis=0).astype(BF16)
    hi, lo = halves(dot(both, table))
    return hi + lo


def expand_rows(z_ref, table, slab, e_ref):
    chans = z_ref.shape[2]
    left = table[:slab]
    pair = 8

    def body(i, carry):
        parts = []
        for k in range(pair):
            z = z_ref[:, :, i * pair + k].reshape(KY, LANES)
            re, im = halves(z)
            both = jnp.concatenate([z, cat(im, -re)], axis=0)
            parts.append(cat(both, both))
        out = dot_nt(left, jnp.concatenate(parts, axis=0)).astype(BF16)
        for k in range(pair):
            e_ref[i * pair + k] = out[:, k * 2 * KY : (k + 1) * 2 * KY]
        return carry

    lax.fori_loop(0, chans // pair, body, 0)


def place():
    devices = lax.axis_size("space")
    me = lax.axis_index("space")
    return devices // 4, me, lax.rem(me, 2), lax.rem(me // 2, 2), me // 4


def peers():
    nz, me, core, mid, z = place()
    across = me + 1 - 2 * core
    beside = me + 2 - 4 * mid
    along = [lax.rem(z + i, nz) for i in range(nz)]
    return across, beside, along, [a * 4 + mid * 2 + core for a in along]


def greet():
    across, beside, _, line = peers()
    barrier = pltpu.get_barrier_semaphore()
    for target in [across, beside] + line[1:]:
        pl.semaphore_signal(barrier, inc=1, device_id={"space": target}, device_id_type=pl.DeviceIdType.MESH)


def greeted():
    pl.semaphore_wait(pltpu.get_barrier_semaphore(), len(peers()[3]) + 1)


class Links:
    def __init__(self, send_sem, recv_sem):
        self.send_sem, self.recv_sem, self.used, self.copies = send_sem, recv_sem, 0, []

    def start(self, src, dst, target):
        copy = pltpu.make_async_remote_copy(
            src_ref=src,
            dst_ref=dst,
            send_sem=self.send_sem.at[self.used],
            recv_sem=self.recv_sem.at[self.used],
            device_id={"space": target},
            device_id_type=pl.DeviceIdType.MESH,
        )
        copy.start()
        self.used += 1
        self.copies.append(copy)
        return copy

    def finish(self):
        for copy in self.copies:
            copy.wait_send()


def exchange_scratch(devices, chans, own, small):
    nz = devices // 4
    count = 5 + 2 * (nz - 1) + (nz + 1 if small else 0)
    shapes = [
        pltpu.VMEM((2, 2, chans, QUARTER, LANES), BF16),
        pltpu.VMEM((2, chans, QUARTER, LANES), BF16),
        pltpu.VMEM((chans, QUARTER, LANES), BF16),
        pltpu.VMEM((chans, QUARTER, LANES), BF16),
        pltpu.VMEM((chans, QUARTER, LANES), F32),
        pltpu.VMEM((nz, own, chans, LANES), F32),
        pltpu.VMEM((nz, own, chans, LANES), BF16),
        pltpu.VMEM((nz, own, chans, LANES), BF16),
        pltpu.VMEM((nz, own, chans, LANES), BF16),
        pltpu.VMEM((2, 2, chans, QUARTER, LANES), BF16),
        pltpu.VMEM((own, chans, chans, LANES), F32),
        pltpu.SemaphoreType.DMA((count,)),
        pltpu.SemaphoreType.DMA((count,)),
        pltpu.SemaphoreType.DMA,
        pltpu.SemaphoreType.DMA,
    ]
    if small:
        shapes += [pltpu.VMEM((4, chans, LANES), F32), pltpu.VMEM((nz, chans, LANES), F32)]
    return shapes


def exchange(scratch, mix, own_ref, z_ref, small_ref=None):
    m, r1, s2, r2, acc, s3f, s3, r3, zg, zt = scratch[:10]
    nz, me, core, mid, z = place()
    across, beside, along, line = peers()
    chans = m.shape[2]
    own = s3.shape[1]
    links = Links(scratch[11], scratch[12])

    first = links.start(m.at[1 - core], r1, across)
    if small_ref is not None:
        sm, rz = scratch[15:17]
        small_first = links.start(sm.at[0], sm.at[1], across)
    first.wait_recv()
    s2[...] = (m[core, 1 - mid].astype(F32) + r1[1 - mid].astype(F32)).astype(BF16)
    second = links.start(s2, r2, beside)
    if small_ref is not None:
        small_first.wait_recv()
        sm[2] = sm[0] + sm[1]
        small_second = links.start(sm.at[2], sm.at[3], beside)
    acc[...] = m[core, mid].astype(F32) + r1[mid].astype(F32)
    second.wait_recv()
    acc[...] += r2[...].astype(F32)
    for a in range(nz):
        for k in range(own):
            block = acc[:, a * own + k, :]
            s3f[a, k] = block
            s3[a, k] = block.astype(BF16)
    sums = [links.start(s3.at[along[i]], r3.at[i], line[i]) for i in range(1, nz)]
    if small_ref is not None:
        small_second.wait_recv()
        rz[z] = sm[2] + sm[3]
        smalls = [links.start(rz.at[z], rz.at[z], line[i]) for i in range(1, nz)]
    for i in range(1, nz):
        sums[i - 1].wait_recv()
    for k in range(own):
        total = s3f[z, k]
        for i in range(1, nz):
            total = total + r3[i, k].astype(F32)
        own_ref[k] = total

    mix(own_ref, zg, z)
    gathered = [links.start(zg.at[z], zg.at[z], line[i]) for i in range(1, nz)]
    if small_ref is not None:
        for copy in smalls:
            copy.wait_recv()
        total = rz[0]
        for i in range(1, nz):
            total = total + rz[i]
        small_ref[...] = total
    for copy in gathered:
        copy.wait_recv()
    for a in range(nz):
        for k in range(own):
            acc[:, a * own + k, :] = zg[a, k].astype(F32)
    zt[core, mid] = acc[...].astype(BF16)
    side = links.start(zt.at[core, mid], zt.at[core, mid], beside)
    near = links.start(zt.at[core, mid], zt.at[core, mid], across)
    side.wait_recv()
    far = links.start(zt.at[core, 1 - mid], zt.at[core, 1 - mid], across)
    near.wait_recv()
    far.wait_recv()
    links.finish()
    z_ref[...] = zt[...]


def mode_gain(me, own, k):
    return jnp.where(me * own + k == 0, 1.0, 2.0).astype(F32)


def swap(value):
    a, b = halves(value)
    return cat(b, a)


def mix_forward(w_ref, me, x_ref, z_ref, z):
    own, chans = w_ref.shape[:2]
    for k in range(own):
        x = x_ref[k]
        x_sw = swap(x)
        first = jnp.zeros(w_ref.shape[2:], F32)
        second = jnp.zeros(w_ref.shape[2:], F32)
        for c in range(chans):
            w = w_ref[k, c]
            first = first + x[c : c + 1] * w
            second = second + x_sw[c : c + 1] * w
        a, b = halves(first)
        c, d = halves(second)
        z_ref[z, k] = (cat(a - b, c + d) * mode_gain(me, own, k)).astype(BF16)


def mix_back(w_ref, me, d_ref, z_ref, z):
    own, chans = w_ref.shape[:2]
    for k in range(own):
        d = d_ref[k] * mode_gain(me, own, k)
        d_ref[k] = d
        d_sw = swap(d)
        firsts, seconds = [], []
        for c in range(chans):
            w = w_ref[k, c]
            firsts.append(jnp.sum(d * w, axis=0, keepdims=True))
            seconds.append(jnp.sum(d_sw * w, axis=0, keepdims=True))
        a, b = halves(jnp.concatenate(firsts, axis=0))
        e, f = halves(jnp.concatenate(seconds, axis=0))
        z_ref[z, k] = cat(a + b, e - f).astype(BF16)


def analysis_kernel(x_ref, bt_ref, cols_ref, w_ref, z_ref, own_ref, cols, *scratch):
    step = pl.program_id(0)
    count, rows, width = x_ref.shape
    m, wv, w_sem, c_sem = scratch[0], scratch[10], scratch[13], scratch[14]
    me = lax.axis_index("space")
    weights = pltpu.make_async_copy(w_ref, wv, w_sem)
    table = pltpu.make_async_copy(cols_ref.at[me], cols, c_sem)

    @pl.when(step == 0)
    def _():
        greet()
        table.start()
        weights.start()
        table.wait()

    flat = x_ref[...].reshape(count * rows, width)
    row_modes = dot(flat, bt_ref[...])
    modes = columns_of([row_modes[c * rows : (c + 1) * rows] for c in range(count)], cols[...]).astype(BF16)
    for c in range(count):
        m[:, :, step * count + c] = modes[c * KY : (c + 1) * KY].reshape(2, 2, QUARTER, LANES)

    @pl.when(step == pl.num_programs(0) - 1)
    def _():
        greeted()
        weights.wait()
        exchange(scratch, functools.partial(mix_forward, wv, me), own_ref, z_ref)


def whole(a):
    return pl.BlockSpec(a.shape, lambda i: (0,) * a.ndim)


def held(shape):
    return pl.BlockSpec(shape, lambda i: (0,) * len(shape))


HBM = pl.BlockSpec(memory_space=pl.ANY)


def analysis(x, bt, cols, weight, devices):
    chans, rows, width = x.shape
    own = weight.shape[0]
    block = 4
    shapes = [
        jax.ShapeDtypeStruct((2, 2, chans, QUARTER, LANES), BF16),
        jax.ShapeDtypeStruct((own, chans, LANES), F32),
    ]
    return pl.pallas_call(
        analysis_kernel,
        grid=(chans // block,),
        in_specs=[pl.BlockSpec((block, rows, width), lambda i: (i, 0, 0)), whole(bt), HBM, HBM],
        out_specs=[held(s.shape) for s in shapes],
        out_shape=shapes,
        scratch_shapes=[pltpu.VMEM(cols.shape[1:], BF16)] + exchange_scratch(devices, chans, own, False),
        compiler_params=pltpu.CompilerParams(vmem_limit_bytes=LIMIT, collective_id=0, has_side_effects=True),
        name="analysis",
    )(x, bt, cols, weight)


def spread(weight, flip, scale):
    chans = weight.shape[0]
    flat = chans * GROUP
    chosen = lax.broadcasted_iota(jnp.int32, (flat, chans), 0) // GROUP == lax.broadcasted_iota(jnp.int32, (flat, chans), 1)
    chosen = jnp.where(chosen, 1.0, 0.0).astype(BF16)
    tall = (dot_nt if flip else dot)(chosen, weight).astype(BF16)
    wide = dot_nt(tall, chosen)
    first = lax.broadcasted_iota(jnp.int32, (flat, flat), 0) % GROUP
    second = lax.broadcasted_iota(jnp.int32, (flat, flat), 1) % GROUP
    return jnp.where(first == second, wide * scale, 0.0).astype(BF16)


def groups_of(value):
    chans, rows, last = value.shape
    return [value[:, g : g + GROUP].reshape(chans * GROUP, last) for g in range(0, rows, GROUP)]


def joined(groups, chans):
    return jnp.concatenate([g.reshape(chans, GROUP, g.shape[-1]) for g in groups], axis=1)


def bias_block(bias):
    hi = bias.astype(BF16).astype(F32)
    mid = (bias - hi).astype(BF16).astype(F32)
    lo = bias - hi - mid
    lane = lax.broadcasted_iota(jnp.int32, bias.shape, 1)
    return jnp.where(lane == 0, hi, jnp.where(lane == 1, mid, jnp.where(lane == 2, lo, 0.0))).astype(BF16)


PHI = (1.5954356609777183, 0.29438608777535386, -0.010105857224310238)


def twice_delta(s, target):
    q = s * s
    p = jnp.minimum(q, 9.0)
    p = (PHI[2] * p + PHI[1]) * p + PHI[0]
    a = 1.0 + jnp.tanh(s * p)
    e = jnp.exp2(q * (-2.0 / math.log(2.0)) + math.log2(4.0 / math.sqrt(2.0 * math.pi)))
    return (s * a - target) * (a + s * e)


def forward_kernel(x_ref, t_ref, z_ref, lw_ref, bias_ref, rb_ref, bt_ref, cols_ref, w_ref,
                   delta_ref, back_ref, dm_ref, small_ref, cols, kron, rows_ref, acc_ref, e_ref, *scratch):
    step = pl.program_id(0)
    chans, rows, width = x_ref.shape
    slab = rows_ref.shape[1]
    half = chans * GROUP
    tile = 512
    m, wv, w_sem, c_sem = scratch[0], scratch[10], scratch[13], scratch[14]
    sm = scratch[15]
    me = lax.axis_index("space")
    weights = pltpu.make_async_copy(w_ref, wv, w_sem)
    table = pltpu.make_async_copy(cols_ref.at[me], cols, c_sem)

    @pl.when(step == 0)
    def _():
        greet()
        table.start()
        weights.start()
        acc_ref[...] = jnp.zeros_like(acc_ref)
        kron[...] = spread(lw_ref[...], True, 0.5)
        table.wait()
        expand_rows(z_ref, cols[...], slab, e_ref)

    band = pl.ds(pl.multiple_of(step * rows, rows), rows)
    e = (e_ref[:, band, :].astype(F32) * 0.5).astype(BF16)
    bias = jnp.broadcast_to((bias_ref[...] * 0.5)[:, None, :], (chans, GROUP, LANES)).reshape(half, LANES)
    bias = bias_block(bias)
    left = [jnp.concatenate([kron[...], group, bias], axis=1) for group in groups_of(e)]
    row_modes = [jnp.zeros((half, bt_ref.shape[1]), F32) for _ in left]
    for start in range(0, width, tile):
        cells = pl.ds(start, tile)
        xs = groups_of(x_ref[:, :, cells])
        targets = groups_of(t_ref[:, :, cells].astype(F32))
        deltas = []
        for lhs, x, target in zip(left, xs, targets):
            s = dot(lhs, jnp.concatenate([x, rb_ref[:, cells]], axis=0))
            deltas.append(twice_delta(s, target))
        delta = joined(deltas, chans).astype(BF16)
        delta_ref[:, :, cells] = delta
        for g, group in enumerate(groups_of(delta)):
            row_modes[g] = row_modes[g] + dot(group, bt_ref[cells, :])
            acc_ref[...] += dot_nt(xs[g], group)
    rows_ref[:, band, :] = joined(row_modes, chans) * 0.5

    @pl.when(step == pl.num_programs(0) - 1)
    def _():
        count = 8

        def body(i, carry):
            modes = columns_of([rows_ref[i * count + k] for k in range(count)], cols[...]).astype(BF16)
            for k in range(count):
                m[:, :, i * count + k] = modes[k * KY : (k + 1) * KY].reshape(2, 2, QUARTER, LANES)
            return carry

        lax.fori_loop(0, chans // count, body, 0)
        first = lax.broadcasted_iota(jnp.int32, (half, half), 0) % GROUP
        second = lax.broadcasted_iota(jnp.int32, (half, half), 1) % GROUP
        kept = jnp.where(first == second, acc_ref[...], 0.0)
        kept = jnp.sum(kept.reshape(chans, GROUP, half), axis=1)
        group = lax.broadcasted_iota(jnp.int32, (half, LANES), 0) // GROUP
        lane = lax.broadcasted_iota(jnp.int32, (half, LANES), 1)
        group = jnp.where(group == lane, 0.5, 0.0).astype(BF16)
        hi = kept.astype(BF16)
        rest = kept - hi.astype(F32)
        lo = rest.astype(BF16)
        last = (rest - lo.astype(F32)).astype(BF16)
        terms = dot(hi, group) + (dot(lo, group) + dot(last, group))
        sums = jnp.sum(rows_ref[...], axis=1)[:, :1]
        lane = lax.broadcasted_iota(jnp.int32, (chans, LANES), 1)
        sm[0] = jnp.where(lane == chans, sums, terms)
        greeted()
        weights.wait()
        exchange(scratch, functools.partial(mix_back, wv, me), dm_ref, back_ref, small_ref)


def forward(x, target, z, local_weight, bias, rb, bt, cols, weight, devices):
    chans, slab, width = x.shape
    own = weight.shape[0]
    half = chans * GROUP
    band = pl.BlockSpec((chans, ROWS, width), lambda i: (0, i, 0))
    shapes = [
        jax.ShapeDtypeStruct(x.shape, BF16),
        jax.ShapeDtypeStruct((2, 2, chans, QUARTER, LANES), BF16),
        jax.ShapeDtypeStruct((own, chans, LANES), F32),
        jax.ShapeDtypeStruct((chans, LANES), F32),
    ]
    return pl.pallas_call(
        forward_kernel,
        grid=(slab // ROWS,),
        in_specs=[band, band, whole(z), whole(local_weight), whole(bias), whole(rb), whole(bt), HBM, HBM],
        out_specs=[band] + [held(s.shape) for s in shapes[1:]],
        out_shape=shapes,
        scratch_shapes=[
            pltpu.VMEM(cols.shape[1:], BF16),
            pltpu.VMEM((half, half), BF16),
            pltpu.VMEM((chans, slab, 2 * KY), F32),
            pltpu.VMEM((half, half), F32),
            pltpu.VMEM((chans, slab, 2 * KY), BF16),
        ] + exchange_scratch(devices, chans, own, True),
        compiler_params=pltpu.CompilerParams(vmem_limit_bytes=LIMIT, collective_id=1, has_side_effects=True),
        name="forward",
    )(x, target, z, local_weight, bias, rb, bt, cols, weight)


def final_kernel(root, cells_count, d_ref, z_ref, lw_ref, rb_ref, cols_ref, xm_ref, dm_ref, small_ref,
                 out_ref, g_ref, local_ref, bias_ref, cols, kron, e_ref, c_sem):
    step = pl.program_id(0)
    chans, rows, width = d_ref.shape
    slab = e_ref.shape[1]
    tile = 512
    pairs = g_ref.shape[0]
    me = lax.axis_index("space")
    table = pltpu.make_async_copy(cols_ref.at[me], cols, c_sem)

    @pl.when(step == 0)
    def _():
        table.start()
        kron[...] = spread(lw_ref[...], False, 0.5)
        small = small_ref[...]
        local_ref[...] = small[:, :chans] * (1.0 / cells_count)
        column = small[:, chans : chans + 1] * (root / cells_count)
        eye = lax.broadcasted_iota(jnp.int32, (chans, chans), 0) == lax.broadcasted_iota(jnp.int32, (chans, chans), 1)
        bias_ref[...] = jnp.sum(jnp.where(eye, column, 0.0), axis=0, keepdims=True)
        table.wait()
        expand_rows(z_ref, cols[...], slab, e_ref)

    e = e_ref[:, pl.ds(pl.multiple_of(step * rows, rows), rows), :]
    left = [cat(kron[...], group) for group in groups_of(e)]
    for start in range(0, width, tile):
        cells = pl.ds(start, tile)
        out = []
        for lhs, d in zip(left, groups_of(d_ref[:, :, cells])):
            out.append(dot(lhs, jnp.concatenate([d, rb_ref[:, cells]], axis=0)))
        out_ref[:, :, cells] = joined(out, chans).astype(BF16)
    for i in range(pairs):
        index = step * pairs + i
        x = xm_ref[pl.ds(index, 1), :]
        re, im = halves(x)
        d = dm_ref[index // chans]
        g_ref[i] = cat(re, re) * d + cat(im, -im) * swap(d)


def final(delta, z, local_weight, rb, cols, own_modes, delta_modes, small, height):
    chans, slab, width = delta.shape
    own = own_modes.shape[0]
    steps = slab // ROWS
    pairs = own * chans // steps
    band = pl.BlockSpec((chans, ROWS, width), lambda i: (0, i, 0))
    own_modes = own_modes.reshape(own * chans, LANES)
    cells_count = height * width
    return pl.pallas_call(
        functools.partial(final_kernel, math.sqrt(cells_count), cells_count),
        grid=(steps,),
        in_specs=[band, whole(z), whole(local_weight), whole(rb), HBM, whole(own_modes), whole(delta_modes), whole(small)],
        out_specs=[
            band,
            pl.BlockSpec((pairs, chans, LANES), lambda i: (i, 0, 0)),
            held((chans, chans)),
            held((1, chans)),
        ],
        out_shape=[
            jax.ShapeDtypeStruct(delta.shape, BF16),
            jax.ShapeDtypeStruct((own * chans, chans, LANES), F32),
            jax.ShapeDtypeStruct((chans, chans), F32),
            jax.ShapeDtypeStruct((1, chans), F32),
        ],
        scratch_shapes=[
            pltpu.VMEM(cols.shape[1:], BF16),
            pltpu.VMEM((chans * GROUP, chans * GROUP), BF16),
            pltpu.VMEM((chans, slab, 2 * KY), BF16),
            pltpu.SemaphoreType.DMA,
        ],
        compiler_params=pltpu.CompilerParams(vmem_limit_bytes=LIMIT),
        name="final",
    )(delta, z, local_weight, rb, cols, own_modes, delta_modes, small)


def per_device(inputs, target, spectral_weight, local_weight, bias_term):
    samples, chans, slab, width = inputs.shape
    devices = lax.axis_size("space")
    height = slab * devices

    table = row_table(height, width, mode_order(devices))
    rb = jnp.asarray(table)
    bt = jnp.asarray(np.ascontiguousarray(table.T))
    ones = np.zeros((LANES, width), ml_dtypes.bfloat16)
    ones[:3] = 1.0
    rb_bias = jnp.asarray(np.concatenate([table, ones]))
    cols = jnp.asarray(column_table(height, devices))
    bias = jnp.broadcast_to(bias_term[:, None], (chans, LANES))

    x = inputs.reshape(chans, slab, width)
    z, own_modes = analysis(x, bt, cols, spectral_weight, devices)
    delta, z, delta_modes, small = forward(
        x, target.reshape(chans, slab, width), z, local_weight, bias, rb_bias, bt, cols, spectral_weight, devices
    )
    grad_input, grad_spectral, grad_local, grad_bias = final(
        delta, z, local_weight, rb, cols, own_modes, delta_modes, small, height
    )
    return (
        grad_input.reshape(inputs.shape),
        grad_spectral.reshape(spectral_weight.shape),
        grad_local,
        grad_bias.reshape(chans),
    )


def solution(mesh):
    return jax.shard_map(
        per_device,
        mesh=mesh,
        in_specs=(
            P("dom", None, "space", None),
            P("dom", None, "space", None),
            P("space", None, None, None),
            P(),
            P(),
        ),
        out_specs=(
            P("dom", None, "space", None),
            P("space", "dom", None, None),
            P("dom", None),
            P("dom"),
        ),
        check_vma=False,
    )
```

```python
import functools
import math

import jax
import jax.numpy as jnp
import ml_dtypes
import numpy as np
from jax import lax
from jax.experimental import pallas as pl
from jax.experimental.pallas import tpu as pltpu
from jax.sharding import PartitionSpec as P

KX = 64
KY = 64
LANES = 2 * KX
QUARTER = KY // 4
LIMIT = 56 * 1024 * 1024
ROWS = 16
BAND = 16
GROUP = 8
F32 = jnp.float32
BF16 = jnp.bfloat16
NT = (((1,), (1,)), ((), ()))
dot = functools.partial(jnp.dot, preferred_element_type=F32)
dot_nt = functools.partial(lax.dot_general, dimension_numbers=NT, preferred_element_type=F32)


def mode_order(devices):
    own = KY // devices
    return np.arange(KY).reshape(devices // 4, 2, 2, own).transpose(2, 1, 0, 3).reshape(-1)


def row_table(height, width, order):
    angles = (order[:, None] * np.arange(width)[None, :] % width) * (2.0 * math.pi / width)
    factor = 1.0 / math.sqrt(height * width)
    return np.concatenate([np.cos(angles) * factor, -np.sin(angles) * factor]).astype(ml_dtypes.bfloat16)


def column_table(height, devices):
    column = np.arange(KX)
    frequency = np.where(column < KX // 2, column, column + height - KX)
    angles = (np.arange(height)[:, None] * frequency[None, :] % height) * (2.0 * math.pi / height)
    cosines, sines = np.cos(angles), np.sin(angles)
    parts = np.stack([np.concatenate([cosines, -sines], 1), np.concatenate([sines, cosines], 1)])
    slab = height // devices
    table = parts.reshape(2, devices, slab, LANES).transpose(1, 0, 2, 3).reshape(devices, 2 * slab, LANES)
    table = table.astype(np.float32)
    hi = table.astype(ml_dtypes.bfloat16)
    lo = (table - hi.astype(np.float32)).astype(ml_dtypes.bfloat16)
    return np.concatenate([hi, lo], axis=2)


def halves(value):
    half = value.shape[-1] // 2
    return value[..., :half], value[..., half:]


def cat(a, b):
    return jnp.concatenate([a, b], axis=-1)


def columns_of(row_modes, table):
    parts = []
    for value in row_modes:
        turned = value.T
        parts.append(cat(turned[:KY], turned[KY:]))
    both = jnp.concatenate(parts, axis=0).astype(BF16)
    hi, lo = halves(dot(both, table))
    return hi + lo


def expand_rows(z_ref, table, slab, e_ref):
    chans = z_ref.shape[2]
    left = table[:slab]
    pair = 8

    def body(i, carry):
        parts = []
        for k in range(pair):
            z = z_ref[:, :, i * pair + k].reshape(KY, LANES)
            re, im = halves(z)
            both = jnp.concatenate([z, cat(im, -re)], axis=0)
            parts.append(cat(both, both))
        out = dot_nt(left, jnp.concatenate(parts, axis=0)).astype(BF16)
        for k in range(pair):
            e_ref[i * pair + k] = out[:, k * 2 * KY : (k + 1) * 2 * KY]
        return carry

    lax.fori_loop(0, chans // pair, body, 0)


def place():
    devices = lax.axis_size("space")
    me = lax.axis_index("space")
    return devices // 4, me, lax.rem(me, 2), lax.rem(me // 2, 2), me // 4


def peers():
    nz, me, core, mid, z = place()
    across = me + 1 - 2 * core
    beside = me + 2 - 4 * mid
    along = [lax.rem(z + i, nz) for i in range(nz)]
    return across, beside, along, [a * 4 + mid * 2 + core for a in along]


def greet():
    across, beside, _, line = peers()
    barrier = pltpu.get_barrier_semaphore()
    for target in [across, beside] + line[1:]:
        pl.semaphore_signal(barrier, inc=1, device_id={"space": target}, device_id_type=pl.DeviceIdType.MESH)


def greeted():
    pl.semaphore_wait(pltpu.get_barrier_semaphore(), len(peers()[3]) + 1)


class Links:
    def __init__(self, send_sem, recv_sem):
        self.send_sem, self.recv_sem, self.used, self.copies = send_sem, recv_sem, 0, []

    def start(self, src, dst, target):
        copy = pltpu.make_async_remote_copy(
            src_ref=src,
            dst_ref=dst,
            send_sem=self.send_sem.at[self.used],
            recv_sem=self.recv_sem.at[self.used],
            device_id={"space": target},
            device_id_type=pl.DeviceIdType.MESH,
        )
        copy.start()
        self.used += 1
        self.copies.append(copy)
        return copy

    def finish(self):
        for copy in self.copies:
            copy.wait_send()


def exchange_scratch(devices, chans, own, small):
    nz = devices // 4
    count = 5 + 2 * (nz - 1) + (nz + 1 if small else 0)
    shapes = [
        pltpu.VMEM((2, 2, chans, QUARTER, LANES), BF16),
        pltpu.VMEM((2, chans, QUARTER, LANES), BF16),
        pltpu.VMEM((chans, QUARTER, LANES), BF16),
        pltpu.VMEM((chans, QUARTER, LANES), BF16),
        pltpu.VMEM((chans, QUARTER, LANES), F32),
        pltpu.VMEM((nz, own, chans, LANES), F32),
        pltpu.VMEM((nz, own, chans, LANES), BF16),
        pltpu.VMEM((nz, own, chans, LANES), BF16),
        pltpu.VMEM((nz, own, chans, LANES), BF16),
        pltpu.VMEM((2, 2, chans, QUARTER, LANES), BF16),
        pltpu.VMEM((own, chans, chans, LANES), F32),
        pltpu.SemaphoreType.DMA((count,)),
        pltpu.SemaphoreType.DMA((count,)),
        pltpu.SemaphoreType.DMA,
        pltpu.SemaphoreType.DMA,
    ]
    if small:
        shapes += [pltpu.VMEM((4, chans, LANES), F32), pltpu.VMEM((nz, chans, LANES), F32)]
    return shapes


def exchange(scratch, mix, own_ref, z_ref, small_ref=None):
    m, r1, s2, r2, acc, s3f, s3, r3, zg, zt = scratch[:10]
    nz, me, core, mid, z = place()
    across, beside, along, line = peers()
    chans = m.shape[2]
    own = s3.shape[1]
    links = Links(scratch[11], scratch[12])

    first = links.start(m.at[1 - core], r1, across)
    if small_ref is not None:
        sm, rz = scratch[15:17]
        small_first = links.start(sm.at[0], sm.at[1], across)
    first.wait_recv()
    s2[...] = (m[core, 1 - mid].astype(F32) + r1[1 - mid].astype(F32)).astype(BF16)
    second = links.start(s2, r2, beside)
    if small_ref is not None:
        small_first.wait_recv()
        sm[2] = sm[0] + sm[1]
        small_second = links.start(sm.at[2], sm.at[3], beside)
    acc[...] = m[core, mid].astype(F32) + r1[mid].astype(F32)
    second.wait_recv()
    acc[...] += r2[...].astype(F32)
    for a in range(nz):
        for k in range(own):
            block = acc[:, a * own + k, :]
            s3f[a, k] = block
            s3[a, k] = block.astype(BF16)
    sums = [links.start(s3.at[along[i]], r3.at[i], line[i]) for i in range(1, nz)]
    if small_ref is not None:
        small_second.wait_recv()
        rz[z] = sm[2] + sm[3]
        smalls = [links.start(rz.at[z], rz.at[z], line[i]) for i in range(1, nz)]
    for i in range(1, nz):
        sums[i - 1].wait_recv()
    for k in range(own):
        total = s3f[z, k]
        for i in range(1, nz):
            total = total + r3[i, k].astype(F32)
        own_ref[k] = total

    mix(own_ref, zg, z)
    gathered = [links.start(zg.at[z], zg.at[z], line[i]) for i in range(1, nz)]
    if small_ref is not None:
        for copy in smalls:
            copy.wait_recv()
        total = rz[0]
        for i in range(1, nz):
            total = total + rz[i]
        small_ref[...] = total
    for copy in gathered:
        copy.wait_recv()
    for a in range(nz):
        for k in range(own):
            acc[:, a * own + k, :] = zg[a, k].astype(F32)
    zt[core, mid] = acc[...].astype(BF16)
    side = links.start(zt.at[core, mid], zt.at[core, mid], beside)
    near = links.start(zt.at[core, mid], zt.at[core, mid], across)
    side.wait_recv()
    far = links.start(zt.at[core, 1 - mid], zt.at[core, 1 - mid], across)
    near.wait_recv()
    far.wait_recv()
    links.finish()
    z_ref[...] = zt[...]


def mode_gain(me, own, k):
    return jnp.where(me * own + k == 0, 1.0, 2.0).astype(F32)


def swap(value):
    a, b = halves(value)
    return cat(b, a)


def mix_forward(w_ref, me, x_ref, z_ref, z):
    own, chans = w_ref.shape[:2]
    for k in range(own):
        x = x_ref[k]
        x_sw = swap(x)
        first = jnp.zeros(w_ref.shape[2:], F32)
        second = jnp.zeros(w_ref.shape[2:], F32)
        for c in range(chans):
            w = w_ref[k, c]
            first = first + x[c : c + 1] * w
            second = second + x_sw[c : c + 1] * w
        a, b = halves(first)
        c, d = halves(second)
        z_ref[z, k] = (cat(a - b, c + d) * mode_gain(me, own, k)).astype(BF16)


def mix_back(w_ref, me, d_ref, z_ref, z):
    own, chans = w_ref.shape[:2]
    for k in range(own):
        d = d_ref[k] * mode_gain(me, own, k)
        d_ref[k] = d
        d_sw = swap(d)
        firsts, seconds = [], []
        for c in range(chans):
            w = w_ref[k, c]
            firsts.append(jnp.sum(d * w, axis=0, keepdims=True))
            seconds.append(jnp.sum(d_sw * w, axis=0, keepdims=True))
        a, b = halves(jnp.concatenate(firsts, axis=0))
        e, f = halves(jnp.concatenate(seconds, axis=0))
        z_ref[z, k] = cat(a + b, e - f).astype(BF16)


def analysis_kernel(x_ref, bt_ref, cols_ref, w_ref, z_ref, own_ref, cols, *scratch):
    step = pl.program_id(0)
    count, rows, width = x_ref.shape
    m, wv, w_sem, c_sem = scratch[0], scratch[10], scratch[13], scratch[14]
    me = lax.axis_index("space")
    weights = pltpu.make_async_copy(w_ref, wv, w_sem)
    table = pltpu.make_async_copy(cols_ref.at[me], cols, c_sem)

    @pl.when(step == 0)
    def _():
        greet()
        table.start()
        weights.start()
        table.wait()

    flat = x_ref[...].reshape(count * rows, width)
    row_modes = dot(flat, bt_ref[...])
    modes = columns_of([row_modes[c * rows : (c + 1) * rows] for c in range(count)], cols[...]).astype(BF16)
    for c in range(count):
        m[:, :, step * count + c] = modes[c * KY : (c + 1) * KY].reshape(2, 2, QUARTER, LANES)

    @pl.when(step == pl.num_programs(0) - 1)
    def _():
        greeted()
        weights.wait()
        exchange(scratch, functools.partial(mix_forward, wv, me), own_ref, z_ref)


def whole(a):
    return pl.BlockSpec(a.shape, lambda i: (0,) * a.ndim)


def held(shape):
    return pl.BlockSpec(shape, lambda i: (0,) * len(shape))


HBM = pl.BlockSpec(memory_space=pl.ANY)


def analysis(x, bt, cols, weight, devices):
    chans, rows, width = x.shape
    own = weight.shape[0]
    block = 8
    shapes = [
        jax.ShapeDtypeStruct((2, 2, chans, QUARTER, LANES), BF16),
        jax.ShapeDtypeStruct((own, chans, LANES), F32),
    ]
    return pl.pallas_call(
        analysis_kernel,
        grid=(chans // block,),
        in_specs=[pl.BlockSpec((block, rows, width), lambda i: (i, 0, 0)), whole(bt), HBM, HBM],
        out_specs=[held(s.shape) for s in shapes],
        out_shape=shapes,
        scratch_shapes=[pltpu.VMEM(cols.shape[1:], BF16)] + exchange_scratch(devices, chans, own, False),
        compiler_params=pltpu.CompilerParams(vmem_limit_bytes=LIMIT, collective_id=0, has_side_effects=True),
        name="analysis",
    )(x, bt, cols, weight)


def spread(weight, flip, scale):
    chans = weight.shape[0]
    flat = chans * GROUP
    chosen = lax.broadcasted_iota(jnp.int32, (flat, chans), 0) // GROUP == lax.broadcasted_iota(jnp.int32, (flat, chans), 1)
    chosen = jnp.where(chosen, 1.0, 0.0).astype(BF16)
    tall = (dot_nt if flip else dot)(chosen, weight).astype(BF16)
    wide = dot_nt(tall, chosen)
    first = lax.broadcasted_iota(jnp.int32, (flat, flat), 0) % GROUP
    second = lax.broadcasted_iota(jnp.int32, (flat, flat), 1) % GROUP
    return jnp.where(first == second, wide * scale, 0.0).astype(BF16)


def groups_of(value):
    chans, rows, last = value.shape
    return [value[:, g : g + GROUP].reshape(chans * GROUP, last) for g in range(0, rows, GROUP)]


def joined(groups, chans):
    return jnp.concatenate([g.reshape(chans, GROUP, g.shape[-1]) for g in groups], axis=1)


def bias_block(bias):
    hi = bias.astype(BF16).astype(F32)
    mid = (bias - hi).astype(BF16).astype(F32)
    lo = bias - hi - mid
    lane = lax.broadcasted_iota(jnp.int32, bias.shape, 1)
    return jnp.where(lane == 0, hi, jnp.where(lane == 1, mid, jnp.where(lane == 2, lo, 0.0))).astype(BF16)


PHI = (1.5954356609777183, 0.29438608777535386, -0.010105857224310238)


def twice_delta(s, target):
    one = lambda value: jnp.asarray(value, BF16)
    q = s * s
    p = jnp.minimum(q, one(9.0))
    p = (one(PHI[2]) * p + one(PHI[1])) * p + one(PHI[0])
    a = one(1.0) + jnp.tanh(s * p)
    e = jnp.exp2(q * one(-2.0 / math.log(2.0)) + one(math.log2(4.0 / math.sqrt(2.0 * math.pi))))
    return (s * a - target) * (a + s * e)


def forward_kernel(x_ref, t_ref, z_ref, lw_ref, bias_ref, rb_ref, bt_ref, cols_ref, w_ref,
                   delta_ref, back_ref, dm_ref, small_ref, cols, kron, rows_ref, acc_ref, e_ref, *scratch):
    step = pl.program_id(0)
    chans, rows, width = x_ref.shape
    slab = rows_ref.shape[1]
    half = chans * GROUP
    tile = 512
    m, wv, w_sem, c_sem = scratch[0], scratch[10], scratch[13], scratch[14]
    sm = scratch[15]
    me = lax.axis_index("space")
    weights = pltpu.make_async_copy(w_ref, wv, w_sem)
    table = pltpu.make_async_copy(cols_ref.at[me], cols, c_sem)

    @pl.when(step == 0)
    def _():
        greet()
        table.start()
        weights.start()
        acc_ref[...] = jnp.zeros_like(acc_ref)
        kron[...] = spread(lw_ref[...], True, 0.5)
        table.wait()
        expand_rows(z_ref, cols[...], slab, e_ref)

    bias = jnp.broadcast_to((bias_ref[...] * 0.5)[:, None, :], (chans, GROUP, LANES)).reshape(half, LANES)
    bias = bias_block(bias)
    def one_band(i, carry):
        first = pl.multiple_of(i * BAND, BAND)
        here = pl.ds(first, BAND)
        band = pl.ds(pl.multiple_of(step * rows + first, BAND), BAND)
        e = (e_ref[:, band, :].astype(F32) * 0.5).astype(BF16)
        left = [cat(group, bias) for group in groups_of(e)]
        deltas = []
        for start in range(0, width, tile):
            cells = pl.ds(start, tile)
            sums = []
            for lhs, x in zip(left, groups_of(x_ref[:, here, cells])):
                sums.append(dot(kron[...], x) + dot(lhs, rb_ref[:, cells]))
            delta = twice_delta(joined(sums, chans).astype(BF16), t_ref[:, here, cells])
            delta_ref[:, here, cells] = delta
            deltas.append(groups_of(delta))
        row_modes = []
        for g, x in enumerate(groups_of(x_ref[:, here, :])):
            delta = jnp.concatenate([d[g] for d in deltas], axis=1)
            both = dot_nt(jnp.concatenate([x, bt_ref[...]], axis=0), delta)
            acc_ref[...] += both[:half]
            row_modes.append(both[half:].T)
        rows_ref[:, band, :] = joined(row_modes, chans) * 0.5
        return carry

    lax.fori_loop(0, rows // BAND, one_band, 0)

    @pl.when(step == pl.num_programs(0) - 1)
    def _():
        count = 8

        def body(i, carry):
            modes = columns_of([rows_ref[i * count + k] for k in range(count)], cols[...]).astype(BF16)
            for k in range(count):
                m[:, :, i * count + k] = modes[k * KY : (k + 1) * KY].reshape(2, 2, QUARTER, LANES)
            return carry

        lax.fori_loop(0, chans // count, body, 0)
        first = lax.broadcasted_iota(jnp.int32, (half, half), 0) % GROUP
        second = lax.broadcasted_iota(jnp.int32, (half, half), 1) % GROUP
        kept = jnp.where(first == second, acc_ref[...], 0.0)
        kept = jnp.sum(kept.reshape(chans, GROUP, half), axis=1)
        group = lax.broadcasted_iota(jnp.int32, (half, LANES), 0) // GROUP
        lane = lax.broadcasted_iota(jnp.int32, (half, LANES), 1)
        group = jnp.where(group == lane, 0.5, 0.0).astype(BF16)
        hi = kept.astype(BF16)
        rest = kept - hi.astype(F32)
        lo = rest.astype(BF16)
        last = (rest - lo.astype(F32)).astype(BF16)
        terms = dot(hi, group) + (dot(lo, group) + dot(last, group))
        sums = jnp.sum(rows_ref[...], axis=1)[:, :1]
        lane = lax.broadcasted_iota(jnp.int32, (chans, LANES), 1)
        sm[0] = jnp.where(lane == chans, sums, terms)
        greeted()
        weights.wait()
        exchange(scratch, functools.partial(mix_back, wv, me), dm_ref, back_ref, small_ref)


def forward(x, target, z, local_weight, bias, rb, bt, cols, weight, devices):
    chans, slab, width = x.shape
    own = weight.shape[0]
    half = chans * GROUP
    band = pl.BlockSpec((chans, ROWS, width), lambda i: (0, i, 0))
    shapes = [
        jax.ShapeDtypeStruct(x.shape, BF16),
        jax.ShapeDtypeStruct((2, 2, chans, QUARTER, LANES), BF16),
        jax.ShapeDtypeStruct((own, chans, LANES), F32),
        jax.ShapeDtypeStruct((chans, LANES), F32),
    ]
    return pl.pallas_call(
        forward_kernel,
        grid=(slab // ROWS,),
        in_specs=[band, band, whole(z), whole(local_weight), whole(bias), whole(rb), whole(bt), HBM, HBM],
        out_specs=[band] + [held(s.shape) for s in shapes[1:]],
        out_shape=shapes,
        scratch_shapes=[
            pltpu.VMEM(cols.shape[1:], BF16),
            pltpu.VMEM((half, half), BF16),
            pltpu.VMEM((chans, slab, 2 * KY), F32),
            pltpu.VMEM((half, half), F32),
            pltpu.VMEM((chans, slab, 2 * KY), BF16),
        ] + exchange_scratch(devices, chans, own, True),
        compiler_params=pltpu.CompilerParams(vmem_limit_bytes=LIMIT, collective_id=1, has_side_effects=True),
        name="forward",
    )(x, target, z, local_weight, bias, rb, bt, cols, weight)


def final_kernel(root, cells_count, d_ref, z_ref, lw_ref, rb_ref, cols_ref, xm_ref, dm_ref, small_ref,
                 out_ref, g_ref, local_ref, bias_ref, cols, kron, e_ref, c_sem):
    step = pl.program_id(0)
    chans, rows, width = d_ref.shape
    slab = e_ref.shape[1]
    tile = 512
    pairs = g_ref.shape[0]
    me = lax.axis_index("space")
    table = pltpu.make_async_copy(cols_ref.at[me], cols, c_sem)

    @pl.when(step == 0)
    def _():
        table.start()
        kron[...] = spread(lw_ref[...], False, 0.5)
        small = small_ref[...]
        local_ref[...] = small[:, :chans] * (1.0 / cells_count)
        column = small[:, chans : chans + 1] * (root / cells_count)
        eye = lax.broadcasted_iota(jnp.int32, (chans, chans), 0) == lax.broadcasted_iota(jnp.int32, (chans, chans), 1)
        bias_ref[...] = jnp.sum(jnp.where(eye, column, 0.0), axis=0, keepdims=True)
        table.wait()
        expand_rows(z_ref, cols[...], slab, e_ref)

    def one_band(i, carry):
        first = pl.multiple_of(i * BAND, BAND)
        here = pl.ds(first, BAND)
        e = e_ref[:, pl.ds(pl.multiple_of(step * rows + first, BAND), BAND), :]
        left = [cat(kron[...], group) for group in groups_of(e)]
        for start in range(0, width, tile):
            cells = pl.ds(start, tile)
            out = []
            for lhs, d in zip(left, groups_of(d_ref[:, here, cells])):
                out.append(dot(lhs, jnp.concatenate([d, rb_ref[:, cells]], axis=0)))
            out_ref[:, here, cells] = joined(out, chans).astype(BF16)
        return carry

    lax.fori_loop(0, rows // BAND, one_band, 0)
    for i in range(pairs):
        index = step * pairs + i
        x = xm_ref[pl.ds(index, 1), :]
        re, im = halves(x)
        d = dm_ref[index // chans]
        g_ref[i] = cat(re, re) * d + cat(im, -im) * swap(d)


def final(delta, z, local_weight, rb, cols, own_modes, delta_modes, small, height):
    chans, slab, width = delta.shape
    own = own_modes.shape[0]
    steps = slab // ROWS
    pairs = own * chans // steps
    band = pl.BlockSpec((chans, ROWS, width), lambda i: (0, i, 0))
    own_modes = own_modes.reshape(own * chans, LANES)
    cells_count = height * width
    return pl.pallas_call(
        functools.partial(final_kernel, math.sqrt(cells_count), cells_count),
        grid=(steps,),
        in_specs=[band, whole(z), whole(local_weight), whole(rb), HBM, whole(own_modes), whole(delta_modes), whole(small)],
        out_specs=[
            band,
            pl.BlockSpec((pairs, chans, LANES), lambda i: (i, 0, 0)),
            held((chans, chans)),
            held((1, chans)),
        ],
        out_shape=[
            jax.ShapeDtypeStruct(delta.shape, BF16),
            jax.ShapeDtypeStruct((own * chans, chans, LANES), F32),
            jax.ShapeDtypeStruct((chans, chans), F32),
            jax.ShapeDtypeStruct((1, chans), F32),
        ],
        scratch_shapes=[
            pltpu.VMEM(cols.shape[1:], BF16),
            pltpu.VMEM((chans * GROUP, chans * GROUP), BF16),
            pltpu.VMEM((chans, slab, 2 * KY), BF16),
            pltpu.SemaphoreType.DMA,
        ],
        compiler_params=pltpu.CompilerParams(vmem_limit_bytes=LIMIT),
        name="final",
    )(delta, z, local_weight, rb, cols, own_modes, delta_modes, small)


def per_device(inputs, target, spectral_weight, local_weight, bias_term):
    samples, chans, slab, width = inputs.shape
    devices = lax.axis_size("space")
    height = slab * devices

    table = row_table(height, width, mode_order(devices))
    rb = jnp.asarray(table)
    bt = jnp.asarray(np.ascontiguousarray(table.T))
    ones = np.zeros((LANES, width), ml_dtypes.bfloat16)
    ones[:3] = 1.0
    rb_bias = jnp.asarray(np.concatenate([table, ones]))
    cols = jnp.asarray(column_table(height, devices))
    bias = jnp.broadcast_to(bias_term[:, None], (chans, LANES))

    x = inputs.reshape(chans, slab, width)
    z, own_modes = analysis(x, bt, cols, spectral_weight, devices)
    delta, z, delta_modes, small = forward(
        x, target.reshape(chans, slab, width), z, local_weight, bias, rb_bias, rb, cols, spectral_weight, devices
    )
    grad_input, grad_spectral, grad_local, grad_bias = final(
        delta, z, local_weight, rb, cols, own_modes, delta_modes, small, height
    )
    return (
        grad_input.reshape(inputs.shape),
        grad_spectral.reshape(spectral_weight.shape),
        grad_local,
        grad_bias.reshape(chans),
    )


def solution(mesh):
    return jax.shard_map(
        per_device,
        mesh=mesh,
        in_specs=(
            P("dom", None, "space", None),
            P("dom", None, "space", None),
            P("space", None, None, None),
            P(),
            P(),
        ),
        out_specs=(
            P("dom", None, "space", None),
            P("space", "dom", None, None),
            P("dom", None),
            P("dom"),
        ),
        check_vma=False,
    )
```

```python
import functools
import math

import jax
import jax.numpy as jnp
import ml_dtypes
import numpy as np
from jax import lax
from jax.experimental import pallas as pl
from jax.experimental.pallas import tpu as pltpu
from jax.sharding import PartitionSpec as P

KX = 64
KY = 64
LANES = 2 * KX
QUARTER = KY // 4
LIMIT = 56 * 1024 * 1024
ROWS = 16
BAND = 16
GROUP = 8
CHUNK = 8
HALF = 16
F32 = jnp.float32
BF16 = jnp.bfloat16
NT = (((1,), (1,)), ((), ()))
dot = functools.partial(jnp.dot, preferred_element_type=F32)
dot_nt = functools.partial(lax.dot_general, dimension_numbers=NT, preferred_element_type=F32)


def mode_order(devices):
    own = KY // devices
    return np.arange(KY).reshape(devices // 4, 2, 2, own).transpose(2, 1, 0, 3).reshape(-1)


def row_table(height, width, order):
    angles = (order[:, None] * np.arange(width)[None, :] % width) * (2.0 * math.pi / width)
    factor = 1.0 / math.sqrt(height * width)
    return np.concatenate([np.cos(angles) * factor, -np.sin(angles) * factor]).astype(ml_dtypes.bfloat16)


def column_table(height, devices):
    column = np.arange(KX)
    frequency = np.where(column < KX // 2, column, column + height - KX)
    angles = (np.arange(height)[:, None] * frequency[None, :] % height) * (2.0 * math.pi / height)
    cosines, sines = np.cos(angles), np.sin(angles)
    parts = np.stack([np.concatenate([cosines, -sines], 1), np.concatenate([sines, cosines], 1)])
    slab = height // devices
    table = parts.reshape(2, devices, slab, LANES).transpose(1, 0, 2, 3).reshape(devices, 2 * slab, LANES)
    table = table.astype(np.float32)
    hi = table.astype(ml_dtypes.bfloat16)
    lo = (table - hi.astype(np.float32)).astype(ml_dtypes.bfloat16)
    return np.concatenate([hi, lo], axis=2)


def halves(value):
    half = value.shape[-1] // 2
    return value[..., :half], value[..., half:]


def cat(a, b):
    return jnp.concatenate([a, b], axis=-1)


def columns_of(row_modes, table):
    parts = []
    for value in row_modes:
        turned = value.T
        parts.append(cat(turned[:KY], turned[KY:]))
    both = jnp.concatenate(parts, axis=0).astype(BF16)
    hi, lo = halves(dot(both, table))
    return hi + lo


def expand_rows(z_ref, table, slab, e_ref):
    chans = z_ref.shape[2]
    left = table[:slab]
    pair = 8

    def body(i, carry):
        parts = []
        for k in range(pair):
            z = z_ref[:, :, i * pair + k].reshape(KY, LANES)
            re, im = halves(z)
            both = jnp.concatenate([z, cat(im, -re)], axis=0)
            parts.append(cat(both, both))
        out = dot_nt(left, jnp.concatenate(parts, axis=0)).astype(BF16)
        for k in range(pair):
            e_ref[i * pair + k] = out[:, k * 2 * KY : (k + 1) * 2 * KY]
        return carry

    lax.fori_loop(0, chans // pair, body, 0)


def place():
    devices = lax.axis_size("space")
    me = lax.axis_index("space")
    return devices // 4, me, lax.rem(me, 2), lax.rem(me // 2, 2), me // 4


def peers():
    nz, me, core, mid, z = place()
    across = me + 1 - 2 * core
    beside = me + 2 - 4 * mid
    along = [lax.rem(z + i, nz) for i in range(nz)]
    return across, beside, along, [a * 4 + mid * 2 + core for a in along]


def greet():
    across, beside, _, line = peers()
    barrier = pltpu.get_barrier_semaphore()
    for target in [across, beside] + line[1:]:
        pl.semaphore_signal(barrier, inc=1, device_id={"space": target}, device_id_type=pl.DeviceIdType.MESH)


def greeted():
    pl.semaphore_wait(pltpu.get_barrier_semaphore(), len(peers()[3]) + 1)


def remote(src, dst, send_sem, recv_sem, target):
    return pltpu.make_async_remote_copy(
        src_ref=src,
        dst_ref=dst,
        send_sem=send_sem,
        recv_sem=recv_sem,
        device_id={"space": target},
        device_id_type=pl.DeviceIdType.MESH,
    )


def exchange_scratch(devices, chans, own, small):
    nz = devices // 4
    parts, wide = chans // CHUNK, chans // HALF
    shapes = [
        pltpu.VMEM((parts, 2, 2, CHUNK, QUARTER, LANES), BF16),
        pltpu.VMEM((parts, 2, CHUNK, QUARTER, LANES), BF16),
        pltpu.VMEM((parts, CHUNK, QUARTER, LANES), BF16),
        pltpu.VMEM((parts, CHUNK, QUARTER, LANES), BF16),
        pltpu.VMEM((parts, CHUNK, QUARTER, LANES), F32),
        pltpu.VMEM((parts, nz, own, CHUNK, LANES), F32),
        pltpu.VMEM((parts, nz, own, CHUNK, LANES), BF16),
        pltpu.VMEM((parts, nz, own, CHUNK, LANES), BF16),
        pltpu.VMEM((wide, nz, own, HALF, LANES), BF16),
        pltpu.VMEM((wide, HALF, QUARTER, LANES), F32),
        pltpu.VMEM((wide, 2, 2, HALF, QUARTER, LANES), BF16),
        pltpu.VMEM((own, chans, chans, LANES), F32),
        pltpu.SemaphoreType.DMA((nz + 1, parts)),
        pltpu.SemaphoreType.DMA((nz + 1, parts)),
        pltpu.SemaphoreType.DMA((nz + 2, wide)),
        pltpu.SemaphoreType.DMA((nz + 2, wide)),
        pltpu.SemaphoreType.DMA,
        pltpu.SemaphoreType.DMA,
    ]
    if small:
        shapes += [
            pltpu.VMEM((4, chans, LANES), F32),
            pltpu.VMEM((nz, chans, LANES), F32),
            pltpu.SemaphoreType.DMA((nz + 1,)),
            pltpu.SemaphoreType.DMA((nz + 1,)),
        ]
    return shapes


class Sums:
    def __init__(self, scratch):
        self.m, self.r1, self.s2, self.r2, self.acc, self.s3f, self.s3, self.r3 = scratch[:8]
        self.send_sem, self.recv_sem = scratch[12:14]
        self.nz, _, self.core, self.mid, self.z = place()
        self.across, self.beside, self.along, self.line = peers()

    def copy(self, stage, c):
        if stage == 0:
            ends = self.m.at[c, 1 - self.core], self.r1.at[c], self.across
        elif stage == 1:
            ends = self.s2.at[c], self.r2.at[c], self.beside
        else:
            i = stage - 1
            ends = self.s3.at[c, self.along[i]], self.r3.at[c, i], self.line[i]
        return remote(ends[0], ends[1], self.send_sem.at[stage, c], self.recv_sem.at[stage, c], ends[2])

    def first(self, c):
        self.copy(0, c).start()

    def second(self, c):
        self.copy(0, c).wait_recv()
        m, r1, core, mid = self.m, self.r1, self.core, self.mid
        self.s2[c] = (m[c, core, 1 - mid].astype(F32) + r1[c, 1 - mid].astype(F32)).astype(BF16)
        self.copy(1, c).start()
        self.acc[c] = m[c, core, mid].astype(F32) + r1[c, mid].astype(F32)

    def third(self, c):
        self.copy(1, c).wait_recv()
        self.acc[c] += self.r2[c].astype(F32)
        own = self.s3.shape[2]
        for a in range(self.nz):
            for k in range(own):
                block = self.acc[c, :, a * own + k, :]
                self.s3f[c, a, k] = block
                self.s3[c, a, k] = block.astype(BF16)
        for i in range(1, self.nz):
            self.copy(1 + i, c).start()

    def advance(self, c):
        self.first(c)
        pl.when(c >= 1)(lambda: self.second(c - 1))
        pl.when(c >= 2)(lambda: self.third(c - 2))

    def close(self, own_ref):
        parts, own = self.m.shape[0], self.s3.shape[2]
        self.second(parts - 1)
        self.third(parts - 2)
        self.third(parts - 1)
        for c in range(parts):
            for i in range(1, self.nz):
                self.copy(1 + i, c).wait_recv()
            for k in range(own):
                total = self.s3f[c, self.z, k]
                for i in range(1, self.nz):
                    total = total + self.r3[c, i, k].astype(F32)
                own_ref[k, c * CHUNK : (c + 1) * CHUNK] = total

    def finish(self):
        for c in range(self.m.shape[0]):
            for stage in range(self.nz + 1):
                self.copy(stage, c).wait_send()


class Small:
    def __init__(self, scratch):
        self.sm, self.rz, self.send_sem, self.recv_sem = scratch[18:22]
        self.nz, _, _, _, self.z = place()
        self.across, self.beside, _, self.line = peers()

    def copy(self, stage):
        if stage == 0:
            ends = self.sm.at[0], self.sm.at[1], self.across
        elif stage == 1:
            ends = self.sm.at[2], self.sm.at[3], self.beside
        else:
            ends = self.rz.at[self.z], self.rz.at[self.z], self.line[stage - 1]
        return remote(ends[0], ends[1], self.send_sem.at[stage], self.recv_sem.at[stage], ends[2])

    def first(self):
        self.copy(0).start()

    def second(self):
        self.copy(0).wait_recv()
        self.sm[2] = self.sm[0] + self.sm[1]
        self.copy(1).start()

    def third(self):
        self.copy(1).wait_recv()
        self.rz[self.z] = self.sm[2] + self.sm[3]
        for i in range(1, self.nz):
            self.copy(1 + i).start()

    def close(self, out_ref):
        for i in range(1, self.nz):
            self.copy(1 + i).wait_recv()
        total = self.rz[0]
        for i in range(1, self.nz):
            total = total + self.rz[i]
        out_ref[...] = total
        for stage in range(self.nz + 1):
            self.copy(stage).wait_send()


def gather(scratch, mix, z_ref, small=None, small_ref=None):
    zg, turn, zt = scratch[8:11]
    send_sem, recv_sem = scratch[14:16]
    nz, _, core, mid, z = place()
    across, beside, _, line = peers()
    own = zg.shape[2]
    wide = zg.shape[0]

    def link(stage, g, src, target):
        return remote(src, src, send_sem.at[stage, g], recv_sem.at[stage, g], target)

    copies = []
    gathered = []
    for g in range(wide):
        mix(g, zg)
        gathered.append([link(i, g, zg.at[g, z], line[i]) for i in range(1, nz)])
        for copy in gathered[g]:
            copy.start()
    if small is not None:
        small.close(small_ref)
    sides = []
    for g in range(wide):
        for copy in gathered[g]:
            copy.wait_recv()
        for a in range(nz):
            for k in range(own):
                turn[g, :, a * own + k, :] = zg[g, a, k].astype(F32)
        zt[g, core, mid] = turn[g].astype(BF16)
        side = link(0, g, zt.at[g, core, mid], beside)
        near = link(nz, g, zt.at[g, core, mid], across)
        side.start()
        near.start()
        sides.append((side, near))
    fars = []
    for g in range(wide):
        sides[g][0].wait_recv()
        far = link(nz + 1, g, zt.at[g, core, 1 - mid], across)
        far.start()
        fars.append(far)
    for g in range(wide):
        sides[g][1].wait_recv()
        fars[g].wait_recv()
        z_ref[:, :, g * HALF : (g + 1) * HALF] = zt[g]
        for copy in gathered[g] + list(sides[g]) + [fars[g]]:
            copy.wait_send()


def mode_gain(me, own, k):
    return jnp.where(me * own + k == 0, 1.0, 2.0).astype(F32)


def swap(value):
    a, b = halves(value)
    return cat(b, a)


def mix_forward(w_ref, me, x_ref, g, z_ref):
    own, chans = w_ref.shape[:2]
    _, _, _, _, z = place()
    for k in range(own):
        x = x_ref[k]
        x_sw = swap(x)
        first = jnp.zeros((HALF, LANES), F32)
        second = jnp.zeros((HALF, LANES), F32)
        for c in range(chans):
            w = w_ref[k, c, g * HALF : (g + 1) * HALF]
            first = first + x[c : c + 1] * w
            second = second + x_sw[c : c + 1] * w
        a, b = halves(first)
        c, d = halves(second)
        z_ref[g, z, k] = (cat(a - b, c + d) * mode_gain(me, own, k)).astype(BF16)


def mix_back(w_ref, me, d_ref, g, z_ref):
    own = w_ref.shape[0]
    _, _, _, _, z = place()
    for k in range(own):
        d = d_ref[k]
        d_sw = swap(d)
        firsts, seconds = [], []
        for c in range(g * HALF, (g + 1) * HALF):
            w = w_ref[k, c]
            firsts.append(jnp.sum(d * w, axis=0, keepdims=True))
            seconds.append(jnp.sum(d_sw * w, axis=0, keepdims=True))
        a, b = halves(jnp.concatenate(firsts, axis=0))
        e, f = halves(jnp.concatenate(seconds, axis=0))
        z_ref[g, z, k] = cat(a + b, e - f).astype(BF16)


def analysis_kernel(x_ref, bt_ref, cols_ref, w_ref, z_ref, own_ref, cols, *scratch):
    step = pl.program_id(0)
    count, rows, width = x_ref.shape
    m, wv, w_sem, c_sem = scratch[0], scratch[11], scratch[16], scratch[17]
    me = lax.axis_index("space")
    weights = pltpu.make_async_copy(w_ref, wv, w_sem)
    table = pltpu.make_async_copy(cols_ref.at[me], cols, c_sem)

    @pl.when(step == 0)
    def _():
        greet()
        table.start()
        weights.start()
        table.wait()

    flat = x_ref[...].reshape(count * rows, width)
    row_modes = dot(flat, bt_ref[...])
    modes = columns_of([row_modes[c * rows : (c + 1) * rows] for c in range(count)], cols[...]).astype(BF16)
    for c in range(count):
        m[step, :, :, c] = modes[c * KY : (c + 1) * KY].reshape(2, 2, QUARTER, LANES)

    @pl.when(step == 0)
    def _():
        greeted()

    sums = Sums(scratch)
    sums.advance(step)

    @pl.when(step == pl.num_programs(0) - 1)
    def _():
        sums.close(own_ref)
        weights.wait()
        gather(scratch, functools.partial(mix_forward, wv, me, own_ref), z_ref)
        sums.finish()


def whole(a):
    return pl.BlockSpec(a.shape, lambda i: (0,) * a.ndim)


def held(shape):
    return pl.BlockSpec(shape, lambda i: (0,) * len(shape))


HBM = pl.BlockSpec(memory_space=pl.ANY)


def analysis(x, bt, cols, weight, devices):
    chans, rows, width = x.shape
    own = weight.shape[0]
    block = CHUNK
    shapes = [
        jax.ShapeDtypeStruct((2, 2, chans, QUARTER, LANES), BF16),
        jax.ShapeDtypeStruct((own, chans, LANES), F32),
    ]
    return pl.pallas_call(
        analysis_kernel,
        grid=(chans // block,),
        in_specs=[pl.BlockSpec((block, rows, width), lambda i: (i, 0, 0)), whole(bt), HBM, HBM],
        out_specs=[held(s.shape) for s in shapes],
        out_shape=shapes,
        scratch_shapes=[pltpu.VMEM(cols.shape[1:], BF16)] + exchange_scratch(devices, chans, own, False),
        compiler_params=pltpu.CompilerParams(vmem_limit_bytes=LIMIT, collective_id=0, has_side_effects=True),
        name="analysis",
    )(x, bt, cols, weight)


def spread(weight, flip, scale):
    chans = weight.shape[0]
    flat = chans * GROUP
    chosen = lax.broadcasted_iota(jnp.int32, (flat, chans), 0) // GROUP == lax.broadcasted_iota(jnp.int32, (flat, chans), 1)
    chosen = jnp.where(chosen, 1.0, 0.0).astype(BF16)
    tall = (dot_nt if flip else dot)(chosen, weight).astype(BF16)
    wide = dot_nt(tall, chosen)
    first = lax.broadcasted_iota(jnp.int32, (flat, flat), 0) % GROUP
    second = lax.broadcasted_iota(jnp.int32, (flat, flat), 1) % GROUP
    return jnp.where(first == second, wide * scale, 0.0).astype(BF16)


def groups_of(value):
    chans, rows, last = value.shape
    return [value[:, g : g + GROUP].reshape(chans * GROUP, last) for g in range(0, rows, GROUP)]


def joined(groups, chans):
    return jnp.concatenate([g.reshape(chans, GROUP, g.shape[-1]) for g in groups], axis=1)


def bias_block(bias):
    hi = bias.astype(BF16).astype(F32)
    mid = (bias - hi).astype(BF16).astype(F32)
    lo = bias - hi - mid
    lane = lax.broadcasted_iota(jnp.int32, bias.shape, 1)
    return jnp.where(lane == 0, hi, jnp.where(lane == 1, mid, jnp.where(lane == 2, lo, 0.0))).astype(BF16)


PHI = (1.5954356609777183, 0.29438608777535386, -0.010105857224310238)


def twice_delta(s, target):
    one = lambda value: jnp.asarray(value, BF16)
    q = s * s
    p = jnp.minimum(q, one(9.0))
    p = (one(PHI[2]) * p + one(PHI[1])) * p + one(PHI[0])
    a = one(1.0) + jnp.tanh(s * p)
    e = jnp.exp2(q * one(-2.0 / math.log(2.0)) + one(math.log2(4.0 / math.sqrt(2.0 * math.pi))))
    return (s * a - target) * (a + s * e)


def forward_kernel(x_ref, t_ref, z_ref, lw_ref, bias_ref, rb_ref, bt_ref, cols_ref, w_ref,
                   delta_ref, back_ref, dm_ref, small_ref, cols, kron, rows_ref, acc_ref, e_ref, *scratch):
    step = pl.program_id(0)
    chans, rows, width = x_ref.shape
    slab = rows_ref.shape[1]
    half = chans * GROUP
    tile = 512
    m, wv, w_sem, c_sem = scratch[0], scratch[11], scratch[16], scratch[17]
    me = lax.axis_index("space")
    weights = pltpu.make_async_copy(w_ref, wv, w_sem)
    table = pltpu.make_async_copy(cols_ref.at[me], cols, c_sem)

    @pl.when(step == 0)
    def _():
        greet()
        table.start()
        weights.start()
        acc_ref[...] = jnp.zeros_like(acc_ref)
        kron[...] = spread(lw_ref[...], True, 0.5)
        table.wait()
        expand_rows(z_ref, cols[...], slab, e_ref)

    bias = jnp.broadcast_to((bias_ref[...] * 0.5)[:, None, :], (chans, GROUP, LANES)).reshape(half, LANES)
    bias = bias_block(bias)
    def one_band(i, carry):
        first = pl.multiple_of(i * BAND, BAND)
        here = pl.ds(first, BAND)
        band = pl.ds(pl.multiple_of(step * rows + first, BAND), BAND)
        e = (e_ref[:, band, :].astype(F32) * 0.5).astype(BF16)
        left = [cat(group, bias) for group in groups_of(e)]
        deltas = []
        for start in range(0, width, tile):
            cells = pl.ds(start, tile)
            sums = []
            for lhs, x in zip(left, groups_of(x_ref[:, here, cells])):
                sums.append(dot(kron[...], x) + dot(lhs, rb_ref[:, cells]))
            delta = twice_delta(joined(sums, chans).astype(BF16), t_ref[:, here, cells])
            delta_ref[:, here, cells] = delta
            deltas.append(groups_of(delta))
        row_modes = []
        for g, x in enumerate(groups_of(x_ref[:, here, :])):
            delta = jnp.concatenate([d[g] for d in deltas], axis=1)
            both = dot_nt(jnp.concatenate([x, bt_ref[...]], axis=0), delta)
            acc_ref[...] += both[:half]
            row_modes.append(both[half:].T)
        rows_ref[:, band, :] = joined(row_modes, chans) * 0.5
        return carry

    lax.fori_loop(0, rows // BAND, one_band, 0)

    @pl.when(step == pl.num_programs(0) - 1)
    def _():
        first = lax.broadcasted_iota(jnp.int32, (half, half), 0) % GROUP
        second = lax.broadcasted_iota(jnp.int32, (half, half), 1) % GROUP
        kept = jnp.where(first == second, acc_ref[...], 0.0)
        kept = jnp.sum(kept.reshape(chans, GROUP, half), axis=1)
        group = lax.broadcasted_iota(jnp.int32, (half, LANES), 0) // GROUP
        lane = lax.broadcasted_iota(jnp.int32, (half, LANES), 1)
        group = jnp.where(group == lane, 0.5, 0.0).astype(BF16)
        hi = kept.astype(BF16)
        rest = kept - hi.astype(F32)
        lo = rest.astype(BF16)
        last = (rest - lo.astype(F32)).astype(BF16)
        terms = dot(hi, group) + (dot(lo, group) + dot(last, group))
        sums = jnp.sum(rows_ref[...], axis=1)[:, :1]
        lane = lax.broadcasted_iota(jnp.int32, (chans, LANES), 1)
        small = Small(scratch)
        small.sm[0] = jnp.where(lane == chans, sums, terms)
        greeted()
        small.first()
        links = Sums(scratch)

        def body(i, carry):
            modes = columns_of([rows_ref[i * CHUNK + k] for k in range(CHUNK)], cols[...]).astype(BF16)
            for k in range(CHUNK):
                m[i, :, :, k] = modes[k * KY : (k + 1) * KY].reshape(2, 2, QUARTER, LANES)
            links.advance(i)
            return carry

        lax.fori_loop(0, chans // CHUNK, body, 0)
        small.second()
        links.close(dm_ref)
        small.third()
        for k in range(dm_ref.shape[0]):
            dm_ref[k] = dm_ref[k] * mode_gain(me, dm_ref.shape[0], k)
        weights.wait()
        gather(scratch, functools.partial(mix_back, wv, me, dm_ref), back_ref, small, small_ref)
        links.finish()


def forward(x, target, z, local_weight, bias, rb, bt, cols, weight, devices):
    chans, slab, width = x.shape
    own = weight.shape[0]
    half = chans * GROUP
    band = pl.BlockSpec((chans, ROWS, width), lambda i: (0, i, 0))
    shapes = [
        jax.ShapeDtypeStruct(x.shape, BF16),
        jax.ShapeDtypeStruct((2, 2, chans, QUARTER, LANES), BF16),
        jax.ShapeDtypeStruct((own, chans, LANES), F32),
        jax.ShapeDtypeStruct((chans, LANES), F32),
    ]
    return pl.pallas_call(
        forward_kernel,
        grid=(slab // ROWS,),
        in_specs=[band, band, whole(z), whole(local_weight), whole(bias), whole(rb), whole(bt), HBM, HBM],
        out_specs=[band] + [held(s.shape) for s in shapes[1:]],
        out_shape=shapes,
        scratch_shapes=[
            pltpu.VMEM(cols.shape[1:], BF16),
            pltpu.VMEM((half, half), BF16),
            pltpu.VMEM((chans, slab, 2 * KY), F32),
            pltpu.VMEM((half, half), F32),
            pltpu.VMEM((chans, slab, 2 * KY), BF16),
        ] + exchange_scratch(devices, chans, own, True),
        compiler_params=pltpu.CompilerParams(vmem_limit_bytes=LIMIT, collective_id=1, has_side_effects=True),
        name="forward",
    )(x, target, z, local_weight, bias, rb, bt, cols, weight)


def final_kernel(root, cells_count, d_ref, z_ref, lw_ref, rb_ref, cols_ref, xm_ref, dm_ref, small_ref,
                 out_ref, g_ref, local_ref, bias_ref, cols, kron, e_ref, c_sem):
    step = pl.program_id(0)
    chans, rows, width = d_ref.shape
    slab = e_ref.shape[1]
    tile = 512
    pairs = g_ref.shape[0]
    me = lax.axis_index("space")
    table = pltpu.make_async_copy(cols_ref.at[me], cols, c_sem)

    @pl.when(step == 0)
    def _():
        table.start()
        kron[...] = spread(lw_ref[...], False, 0.5)
        small = small_ref[...]
        local_ref[...] = small[:, :chans] * (1.0 / cells_count)
        column = small[:, chans : chans + 1] * (root / cells_count)
        eye = lax.broadcasted_iota(jnp.int32, (chans, chans), 0) == lax.broadcasted_iota(jnp.int32, (chans, chans), 1)
        bias_ref[...] = jnp.sum(jnp.where(eye, column, 0.0), axis=0, keepdims=True)
        table.wait()
        expand_rows(z_ref, cols[...], slab, e_ref)

    def one_band(i, carry):
        first = pl.multiple_of(i * BAND, BAND)
        here = pl.ds(first, BAND)
        e = e_ref[:, pl.ds(pl.multiple_of(step * rows + first, BAND), BAND), :]
        left = [cat(kron[...], group) for group in groups_of(e)]
        for start in range(0, width, tile):
            cells = pl.ds(start, tile)
            out = []
            for lhs, d in zip(left, groups_of(d_ref[:, here, cells])):
                out.append(dot(lhs, jnp.concatenate([d, rb_ref[:, cells]], axis=0)))
            out_ref[:, here, cells] = joined(out, chans).astype(BF16)
        return carry

    lax.fori_loop(0, rows // BAND, one_band, 0)
    for i in range(pairs):
        index = step * pairs + i
        x = xm_ref[pl.ds(index, 1), :]
        re, im = halves(x)
        d = dm_ref[index // chans]
        g_ref[i] = cat(re, re) * d + cat(im, -im) * swap(d)


def final(delta, z, local_weight, rb, cols, own_modes, delta_modes, small, height):
    chans, slab, width = delta.shape
    own = own_modes.shape[0]
    steps = slab // ROWS
    pairs = own * chans // steps
    band = pl.BlockSpec((chans, ROWS, width), lambda i: (0, i, 0))
    own_modes = own_modes.reshape(own * chans, LANES)
    cells_count = height * width
    return pl.pallas_call(
        functools.partial(final_kernel, math.sqrt(cells_count), cells_count),
        grid=(steps,),
        in_specs=[band, whole(z), whole(local_weight), whole(rb), HBM, whole(own_modes), whole(delta_modes), whole(small)],
        out_specs=[
            band,
            pl.BlockSpec((pairs, chans, LANES), lambda i: (i, 0, 0)),
            held((chans, chans)),
            held((1, chans)),
        ],
        out_shape=[
            jax.ShapeDtypeStruct(delta.shape, BF16),
            jax.ShapeDtypeStruct((own * chans, chans, LANES), F32),
            jax.ShapeDtypeStruct((chans, chans), F32),
            jax.ShapeDtypeStruct((1, chans), F32),
        ],
        scratch_shapes=[
            pltpu.VMEM(cols.shape[1:], BF16),
            pltpu.VMEM((chans * GROUP, chans * GROUP), BF16),
            pltpu.VMEM((chans, slab, 2 * KY), BF16),
            pltpu.SemaphoreType.DMA,
        ],
        compiler_params=pltpu.CompilerParams(vmem_limit_bytes=LIMIT),
        name="final",
    )(delta, z, local_weight, rb, cols, own_modes, delta_modes, small)


def per_device(inputs, target, spectral_weight, local_weight, bias_term):
    samples, chans, slab, width = inputs.shape
    devices = lax.axis_size("space")
    height = slab * devices

    table = row_table(height, width, mode_order(devices))
    rb = jnp.asarray(table)
    bt = jnp.asarray(np.ascontiguousarray(table.T))
    ones = np.zeros((LANES, width), ml_dtypes.bfloat16)
    ones[:3] = 1.0
    rb_bias = jnp.asarray(np.concatenate([table, ones]))
    cols = jnp.asarray(column_table(height, devices))
    bias = jnp.broadcast_to(bias_term[:, None], (chans, LANES))

    x = inputs.reshape(chans, slab, width)
    z, own_modes = analysis(x, bt, cols, spectral_weight, devices)
    delta, z, delta_modes, small = forward(
        x, target.reshape(chans, slab, width), z, local_weight, bias, rb_bias, rb, cols, spectral_weight, devices
    )
    grad_input, grad_spectral, grad_local, grad_bias = final(
        delta, z, local_weight, rb, cols, own_modes, delta_modes, small, height
    )
    return (
        grad_input.reshape(inputs.shape),
        grad_spectral.reshape(spectral_weight.shape),
        grad_local,
        grad_bias.reshape(chans),
    )


def solution(mesh):
    return jax.shard_map(
        per_device,
        mesh=mesh,
        in_specs=(
            P("dom", None, "space", None),
            P("dom", None, "space", None),
            P("space", None, None, None),
            P(),
            P(),
        ),
        out_specs=(
            P("dom", None, "space", None),
            P("space", "dom", None, None),
            P("dom", None),
            P("dom"),
        ),
        check_vma=False,
    )
```

```python
import functools
import math

import jax
import jax.numpy as jnp
import ml_dtypes
import numpy as np
from jax import lax
from jax.experimental import pallas as pl
from jax.experimental.pallas import tpu as pltpu
from jax.sharding import PartitionSpec as P

KX = 64
KY = 64
LANES = 2 * KX
QUARTER = KY // 4
LIMIT = 56 * 1024 * 1024
ROWS = 16
BAND = 16
GROUP = 8
CHUNK = 8
HALF = 16
THIRD = 1
MIX = 4
LAST_ROWS = 32
F32 = jnp.float32
BF16 = jnp.bfloat16
NT = (((1,), (1,)), ((), ()))
dot = functools.partial(jnp.dot, preferred_element_type=F32)
dot_nt = functools.partial(lax.dot_general, dimension_numbers=NT, preferred_element_type=F32)


def mode_order(devices):
    own = KY // devices
    return np.arange(KY).reshape(devices // 4, 2, 2, own).transpose(2, 1, 0, 3).reshape(-1)


def row_table(height, width, order):
    angles = (order[:, None] * np.arange(width)[None, :] % width) * (2.0 * math.pi / width)
    factor = 1.0 / math.sqrt(height * width)
    return np.concatenate([np.cos(angles) * factor, -np.sin(angles) * factor]).astype(ml_dtypes.bfloat16)


def column_table(height, devices):
    column = np.arange(KX)
    frequency = np.where(column < KX // 2, column, column + height - KX)
    angles = (np.arange(height)[:, None] * frequency[None, :] % height) * (2.0 * math.pi / height)
    cosines, sines = np.cos(angles), np.sin(angles)
    parts = np.stack([np.concatenate([cosines, -sines], 1), np.concatenate([sines, cosines], 1)])
    slab = height // devices
    table = parts.reshape(2, devices, slab, LANES).transpose(1, 0, 2, 3).reshape(devices, 2 * slab, LANES)
    table = table.astype(np.float32)
    hi = table.astype(ml_dtypes.bfloat16)
    lo = (table - hi.astype(np.float32)).astype(ml_dtypes.bfloat16)
    return np.concatenate([hi, lo], axis=2)


def halves(value):
    half = value.shape[-1] // 2
    return value[..., :half], value[..., half:]


def cat(a, b):
    return jnp.concatenate([a, b], axis=-1)


def columns_of(row_modes, table):
    parts = []
    for value in row_modes:
        turned = value.T
        parts.append(cat(turned[:KY], turned[KY:]))
    both = jnp.concatenate(parts, axis=0).astype(BF16)
    hi, lo = halves(dot(both, table))
    return hi + lo


def expand_rows(z_ref, table, slab, e_ref):
    chans = z_ref.shape[2]
    left = table[:slab]
    pair = 8

    def body(i, carry):
        parts = []
        for k in range(pair):
            z = z_ref[:, :, i * pair + k].reshape(KY, LANES)
            re, im = halves(z)
            both = jnp.concatenate([z, cat(im, -re)], axis=0)
            parts.append(cat(both, both))
        out = dot_nt(left, jnp.concatenate(parts, axis=0)).astype(BF16)
        for k in range(pair):
            e_ref[i * pair + k] = out[:, k * 2 * KY : (k + 1) * 2 * KY]
        return carry

    lax.fori_loop(0, chans // pair, body, 0)


def place():
    devices = lax.axis_size("space")
    me = lax.axis_index("space")
    return devices // 4, me, lax.rem(me, 2), lax.rem(me // 2, 2), me // 4


def peers():
    nz, me, core, mid, z = place()
    across = me + 1 - 2 * core
    beside = me + 2 - 4 * mid
    along = [lax.rem(z + i, nz) for i in range(nz)]
    return across, beside, along, [a * 4 + mid * 2 + core for a in along]


def greet():
    across, beside, _, line = peers()
    barrier = pltpu.get_barrier_semaphore()
    for target in [across, beside] + line[1:]:
        pl.semaphore_signal(barrier, inc=1, device_id={"space": target}, device_id_type=pl.DeviceIdType.MESH)


def greeted():
    pl.semaphore_wait(pltpu.get_barrier_semaphore(), len(peers()[3]) + 1)


def remote(src, dst, send_sem, recv_sem, target):
    return pltpu.make_async_remote_copy(
        src_ref=src,
        dst_ref=dst,
        send_sem=send_sem,
        recv_sem=recv_sem,
        device_id={"space": target},
        device_id_type=pl.DeviceIdType.MESH,
    )


def exchange_scratch(devices, chans, own, small):
    nz = devices // 4
    parts, wide = chans // CHUNK, chans // HALF
    shapes = [
        pltpu.VMEM((parts, 2, 2, CHUNK, QUARTER, LANES), BF16),
        pltpu.VMEM((parts, 2, CHUNK, QUARTER, LANES), BF16),
        pltpu.VMEM((parts, CHUNK, QUARTER, LANES), BF16),
        pltpu.VMEM((parts, CHUNK, QUARTER, LANES), BF16),
        pltpu.VMEM((parts, CHUNK, QUARTER, LANES), F32),
        pltpu.VMEM((parts, nz, own, CHUNK, LANES), F32),
        pltpu.VMEM((parts, nz, own, CHUNK, LANES), BF16),
        pltpu.VMEM((parts, nz, own, CHUNK, LANES), BF16),
        pltpu.VMEM((wide, nz, own, HALF, LANES), BF16),
        pltpu.VMEM((wide, HALF, QUARTER, LANES), F32),
        pltpu.VMEM((wide, 2, 2, HALF, QUARTER, LANES), BF16),
        pltpu.VMEM((own, chans, chans, LANES), F32),
        pltpu.SemaphoreType.DMA((nz + 1, parts)),
        pltpu.SemaphoreType.DMA((nz + 1, parts)),
        pltpu.SemaphoreType.DMA((nz + 2, wide)),
        pltpu.SemaphoreType.DMA((nz + 2, wide)),
        pltpu.SemaphoreType.DMA,
        pltpu.SemaphoreType.DMA,
    ]
    if small:
        shapes += [
            pltpu.VMEM((4, chans, LANES), F32),
            pltpu.VMEM((nz, chans, LANES), F32),
            pltpu.SemaphoreType.DMA((nz + 1,)),
            pltpu.SemaphoreType.DMA((nz + 1,)),
        ]
    return shapes


class Sums:
    def __init__(self, scratch):
        self.m, self.r1, self.s2, self.r2, self.acc, self.s3f, self.s3, self.r3 = scratch[:8]
        self.send_sem, self.recv_sem = scratch[12:14]
        self.nz, _, self.core, self.mid, self.z = place()
        self.across, self.beside, self.along, self.line = peers()

    def copy(self, stage, c):
        if stage == 0:
            ends = self.m.at[c, 1 - self.core], self.r1.at[c], self.across
        elif stage == 1:
            ends = self.s2.at[c], self.r2.at[c], self.beside
        else:
            i = stage - 1
            ends = self.s3.at[c, self.along[i]], self.r3.at[c, i], self.line[i]
        return remote(ends[0], ends[1], self.send_sem.at[stage, c], self.recv_sem.at[stage, c], ends[2])

    def first(self, c):
        self.copy(0, c).start()

    def second(self, c):
        self.copy(0, c).wait_recv()
        m, r1, core, mid = self.m, self.r1, self.core, self.mid
        self.s2[c] = (m[c, core, 1 - mid].astype(F32) + r1[c, 1 - mid].astype(F32)).astype(BF16)
        self.copy(1, c).start()
        self.acc[c] = m[c, core, mid].astype(F32) + r1[c, mid].astype(F32)

    def third(self, c):
        self.copy(1, c).wait_recv()
        self.acc[c] += self.r2[c].astype(F32)
        own = self.s3.shape[2]
        for a in range(self.nz):
            for k in range(own):
                block = self.acc[c, :, a * own + k, :]
                self.s3f[c, a, k] = block
                self.s3[c, a, k] = block.astype(BF16)
        for i in range(1, self.nz):
            self.copy(1 + i, c).start()

    def advance(self, c):
        self.first(c)
        pl.when(c >= 1)(lambda: self.second(c - 1))
        pl.when(c >= 2)(lambda: self.third(c - 2))

    def close(self, own_ref):
        parts, own = self.m.shape[0], self.s3.shape[2]
        for c in range(parts):
            for i in range(1, self.nz):
                self.copy(1 + i, c).wait_recv()
            for k in range(own):
                total = self.s3f[c, self.z, k]
                for i in range(1, self.nz):
                    total = total + self.r3[c, i, k].astype(F32)
                own_ref[k, c * CHUNK : (c + 1) * CHUNK] = total

    def finish(self):
        for c in range(self.m.shape[0]):
            for stage in range(self.nz + 1):
                self.copy(stage, c).wait_send()


class Small:
    def __init__(self, scratch):
        self.sm, self.rz, self.send_sem, self.recv_sem = scratch[18:22]
        self.nz, _, _, _, self.z = place()
        self.across, self.beside, _, self.line = peers()

    def copy(self, stage):
        if stage == 0:
            ends = self.sm.at[0], self.sm.at[1], self.across
        elif stage == 1:
            ends = self.sm.at[2], self.sm.at[3], self.beside
        else:
            ends = self.rz.at[self.z], self.rz.at[self.z], self.line[stage - 1]
        return remote(ends[0], ends[1], self.send_sem.at[stage], self.recv_sem.at[stage], ends[2])

    def first(self):
        self.copy(0).start()

    def second(self):
        self.copy(0).wait_recv()
        self.sm[2] = self.sm[0] + self.sm[1]
        self.copy(1).start()

    def third(self):
        self.copy(1).wait_recv()
        self.rz[self.z] = self.sm[2] + self.sm[3]
        for i in range(1, self.nz):
            self.copy(1 + i).start()

    def close(self, out_ref):
        for i in range(1, self.nz):
            self.copy(1 + i).wait_recv()
        total = self.rz[0]
        for i in range(1, self.nz):
            total = total + self.rz[i]
        out_ref[...] = total
        for stage in range(self.nz + 1):
            self.copy(stage).wait_send()


class Gather:
    def __init__(self, scratch):
        self.zg, self.turn, self.zt = scratch[8:11]
        self.send_sem, self.recv_sem = scratch[14:16]
        self.nz, _, self.core, self.mid, self.z = place()
        self.across, self.beside, _, self.line = peers()
        self.wide = self.zg.shape[0]

    def copy(self, stage, g):
        if stage == 0:
            src, target = self.zt.at[g, self.core, self.mid], self.beside
        elif stage < self.nz:
            src, target = self.zg.at[g, self.z], self.line[stage]
        elif stage == self.nz:
            src, target = self.zt.at[g, self.core, self.mid], self.across
        else:
            src, target = self.zt.at[g, self.core, 1 - self.mid], self.across
        return remote(src, src, self.send_sem.at[stage, g], self.recv_sem.at[stage, g], target)

    def first(self, mix):
        for g in range(self.wide):
            mix(g, self.zg)
            for i in range(1, self.nz):
                self.copy(i, g).start()

    def close(self, z_ref):
        zg, turn, zt = self.zg, self.turn, self.zt
        own = zg.shape[2]
        for g in range(self.wide):
            for i in range(1, self.nz):
                self.copy(i, g).wait_recv()
            for a in range(self.nz):
                for k in range(own):
                    turn[g, :, a * own + k, :] = zg[g, a, k].astype(F32)
            zt[g, self.core, self.mid] = turn[g].astype(BF16)
            self.copy(0, g).start()
            self.copy(self.nz, g).start()
        for g in range(self.wide):
            self.copy(0, g).wait_recv()
            self.copy(self.nz + 1, g).start()
        for g in range(self.wide):
            self.copy(self.nz, g).wait_recv()
            self.copy(self.nz + 1, g).wait_recv()
            z_ref[:, :, g * HALF : (g + 1) * HALF] = zt[g]
            for stage in range(self.nz + 2):
                self.copy(stage, g).wait_send()


def mode_gain(me, own, k):
    return jnp.where(me * own + k == 0, 1.0, 2.0).astype(F32)


def swap(value):
    a, b = halves(value)
    return cat(b, a)


def mix_forward(w_ref, me, x_ref, g, z_ref):
    own, chans = w_ref.shape[:2]
    _, _, _, _, z = place()
    for k in range(own):
        x = x_ref[k]
        x_sw = swap(x)
        first = jnp.zeros((HALF, LANES), F32)
        second = jnp.zeros((HALF, LANES), F32)
        for c in range(chans):
            w = w_ref[k, c, g * HALF : (g + 1) * HALF]
            first = first + x[c : c + 1] * w
            second = second + x_sw[c : c + 1] * w
        a, b = halves(first)
        c, d = halves(second)
        z_ref[g, z, k] = (cat(a - b, c + d) * mode_gain(me, own, k)).astype(BF16)


def mix_back(w_ref, me, d_ref, g, z_ref):
    own = w_ref.shape[0]
    _, _, _, _, z = place()
    for k in range(own):
        d = d_ref[k]
        d_sw = swap(d)
        firsts, seconds = [], []
        for c in range(g * HALF, (g + 1) * HALF):
            w = w_ref[k, c]
            firsts.append(jnp.sum(d * w, axis=0, keepdims=True))
            seconds.append(jnp.sum(d_sw * w, axis=0, keepdims=True))
        a, b = halves(jnp.concatenate(firsts, axis=0))
        e, f = halves(jnp.concatenate(seconds, axis=0))
        z_ref[g, z, k] = cat(a + b, e - f).astype(BF16)


def analysis_kernel(x_ref, bt_ref, cols_ref, w_ref, z_ref, own_ref, cols, *scratch):
    step = pl.program_id(0)
    count, rows, width = x_ref.shape
    m, wv, w_sem, c_sem = scratch[0], scratch[11], scratch[16], scratch[17]
    me = lax.axis_index("space")
    weights = pltpu.make_async_copy(w_ref, wv, w_sem)
    table = pltpu.make_async_copy(cols_ref.at[me], cols, c_sem)

    @pl.when(step == 0)
    def _():
        greet()
        table.start()
        weights.start()
        table.wait()

    flat = x_ref[...].reshape(count * rows, width)
    row_modes = dot(flat, bt_ref[...])
    modes = columns_of([row_modes[c * rows : (c + 1) * rows] for c in range(count)], cols[...]).astype(BF16)
    for c in range(count):
        m[step, :, :, c] = modes[c * KY : (c + 1) * KY].reshape(2, 2, QUARTER, LANES)

    @pl.when(step == 0)
    def _():
        greeted()

    sums = Sums(scratch)
    sums.advance(step)

    @pl.when(step == pl.num_programs(0) - 1)
    def _():
        sums.second(step)
        sums.third(step - 1)
        sums.third(step)
        sums.close(own_ref)
        weights.wait()
        gather = Gather(scratch)
        gather.first(functools.partial(mix_forward, wv, me, own_ref))
        gather.close(z_ref)
        sums.finish()


def whole(a):
    return pl.BlockSpec(a.shape, lambda i: (0,) * a.ndim)


def held(shape):
    return pl.BlockSpec(shape, lambda i: (0,) * len(shape))


HBM = pl.BlockSpec(memory_space=pl.ANY)


def analysis(x, bt, cols, weight, devices):
    chans, rows, width = x.shape
    own = weight.shape[0]
    block = CHUNK
    shapes = [
        jax.ShapeDtypeStruct((2, 2, chans, QUARTER, LANES), BF16),
        jax.ShapeDtypeStruct((own, chans, LANES), F32),
    ]
    return pl.pallas_call(
        analysis_kernel,
        grid=(chans // block,),
        in_specs=[pl.BlockSpec((block, rows, width), lambda i: (i, 0, 0)), whole(bt), HBM, HBM],
        out_specs=[held(s.shape) for s in shapes],
        out_shape=shapes,
        scratch_shapes=[pltpu.VMEM(cols.shape[1:], BF16)] + exchange_scratch(devices, chans, own, False),
        compiler_params=pltpu.CompilerParams(vmem_limit_bytes=LIMIT, collective_id=0, has_side_effects=True),
        name="analysis",
    )(x, bt, cols, weight)


def spread(weight, flip, scale):
    chans = weight.shape[0]
    flat = chans * GROUP
    chosen = lax.broadcasted_iota(jnp.int32, (flat, chans), 0) // GROUP == lax.broadcasted_iota(jnp.int32, (flat, chans), 1)
    chosen = jnp.where(chosen, 1.0, 0.0).astype(BF16)
    tall = (dot_nt if flip else dot)(chosen, weight).astype(BF16)
    wide = dot_nt(tall, chosen)
    first = lax.broadcasted_iota(jnp.int32, (flat, flat), 0) % GROUP
    second = lax.broadcasted_iota(jnp.int32, (flat, flat), 1) % GROUP
    return jnp.where(first == second, wide * scale, 0.0).astype(BF16)


def groups_of(value):
    chans, rows, last = value.shape
    return [value[:, g : g + GROUP].reshape(chans * GROUP, last) for g in range(0, rows, GROUP)]


def joined(groups, chans):
    return jnp.concatenate([g.reshape(chans, GROUP, g.shape[-1]) for g in groups], axis=1)


def bias_block(bias):
    hi = bias.astype(BF16).astype(F32)
    mid = (bias - hi).astype(BF16).astype(F32)
    lo = bias - hi - mid
    lane = lax.broadcasted_iota(jnp.int32, bias.shape, 1)
    return jnp.where(lane == 0, hi, jnp.where(lane == 1, mid, jnp.where(lane == 2, lo, 0.0))).astype(BF16)


PHI = (1.5954356609777183, 0.29438608777535386, -0.010105857224310238)


def twice_delta(s, target):
    one = lambda value: jnp.asarray(value, BF16)
    q = s * s
    p = jnp.minimum(q, one(9.0))
    p = (one(PHI[2]) * p + one(PHI[1])) * p + one(PHI[0])
    a = one(1.0) + jnp.tanh(s * p)
    e = jnp.exp2(q * one(-2.0 / math.log(2.0)) + one(math.log2(4.0 / math.sqrt(2.0 * math.pi))))
    return (s * a - target) * (a + s * e)


def forward_kernel(x_ref, t_ref, z_ref, lw_ref, bias_ref, rb_ref, bt_ref, cols_ref, w_ref,
                   part_ref, back_ref, dm_ref, small_ref, cols, kron, kron_back, delta_ref, rows_ref, acc_ref, e_ref,
                   *scratch):
    step = pl.program_id(0)
    bands = pl.num_programs(0) // 2
    chans, rows, width = x_ref.shape
    slab = rows_ref.shape[1]
    half = chans * GROUP
    tile = 512
    m, wv, w_sem, c_sem = scratch[0], scratch[11], scratch[16], scratch[17]
    me = lax.axis_index("space")
    weights = pltpu.make_async_copy(w_ref, wv, w_sem)
    table = pltpu.make_async_copy(cols_ref.at[me], cols, c_sem)

    @pl.when(step == 0)
    def _():
        greet()
        table.start()
        weights.start()
        acc_ref[...] = jnp.zeros_like(acc_ref)
        kron[...] = spread(lw_ref[...], True, 0.5)
        kron_back[...] = spread(lw_ref[...], False, 0.5)
        table.wait()
        expand_rows(z_ref, cols[...], slab, e_ref)

    @pl.when(step < bands)
    def _():
        bias = jnp.broadcast_to((bias_ref[...] * 0.5)[:, None, :], (chans, GROUP, LANES)).reshape(half, LANES)
        bias = bias_block(bias)
        band = pl.ds(pl.multiple_of(step * rows, rows), rows)
        e = (e_ref[:, band, :].astype(F32) * 0.5).astype(BF16)
        left = [cat(group, bias) for group in groups_of(e)]
        deltas = []
        for start in range(0, width, tile):
            cells = pl.ds(start, tile)
            sums = []
            for lhs, x in zip(left, groups_of(x_ref[:, :, cells])):
                sums.append(dot(kron[...], x) + dot(lhs, rb_ref[:, cells]))
            delta = twice_delta(joined(sums, chans).astype(BF16), t_ref[:, :, cells])
            delta_ref[:, band, cells] = delta
            deltas.append(groups_of(delta))
        row_modes = []
        for g, x in enumerate(groups_of(x_ref[...])):
            delta = jnp.concatenate([d[g] for d in deltas], axis=1)
            both = dot_nt(jnp.concatenate([x, bt_ref[...]], axis=0), delta)
            acc_ref[...] += both[:half]
            row_modes.append(both[half:].T)
        rows_ref[:, band, :] = joined(row_modes, chans) * 0.5

    @pl.when(step >= bands)
    def _():
        band = pl.ds(pl.multiple_of((step - bands) * rows, rows), rows)
        for start in range(0, width, tile):
            cells = pl.ds(start, tile)
            out = [dot(kron_back[...], d) for d in groups_of(delta_ref[:, band, cells])]
            part_ref[:, :, cells] = joined(out, chans).astype(BF16)

    small = Small(scratch)
    links = Sums(scratch)
    gather = Gather(scratch)
    own = dm_ref.shape[0]
    chunks = chans // CHUNK

    @pl.when(step == bands - 1)
    def _():
        first = lax.broadcasted_iota(jnp.int32, (half, half), 0) % GROUP
        second = lax.broadcasted_iota(jnp.int32, (half, half), 1) % GROUP
        kept = jnp.where(first == second, acc_ref[...], 0.0)
        kept = jnp.sum(kept.reshape(chans, GROUP, half), axis=1)
        group = lax.broadcasted_iota(jnp.int32, (half, LANES), 0) // GROUP
        lane = lax.broadcasted_iota(jnp.int32, (half, LANES), 1)
        group = jnp.where(group == lane, 0.5, 0.0).astype(BF16)
        hi = kept.astype(BF16)
        rest = kept - hi.astype(F32)
        lo = rest.astype(BF16)
        last = (rest - lo.astype(F32)).astype(BF16)
        terms = dot(hi, group) + (dot(lo, group) + dot(last, group))
        sums = jnp.sum(rows_ref[...], axis=1)[:, :1]
        lane = lax.broadcasted_iota(jnp.int32, (chans, LANES), 1)
        small.sm[0] = jnp.where(lane == chans, sums, terms)
        greeted()
        small.first()

        def body(i, carry):
            modes = columns_of([rows_ref[i * CHUNK + k] for k in range(CHUNK)], cols[...]).astype(BF16)
            for k in range(CHUNK):
                m[i, :, :, k] = modes[k * KY : (k + 1) * KY].reshape(2, 2, QUARTER, LANES)
            links.first(i)
            pl.when(i >= 1)(lambda: links.second(i - 1))
            return carry

        lax.fori_loop(0, chunks, body, 0)
        links.second(chunks - 1)
        small.second()

    @pl.when(step == bands + jnp.minimum(THIRD, bands - 1))
    def _():
        for c in range(chunks):
            links.third(c)
        small.third()

    @pl.when(step == bands + jnp.minimum(MIX, bands - 1))
    def _():
        links.close(dm_ref)
        for k in range(own):
            dm_ref[k] = dm_ref[k] * mode_gain(me, own, k)
        weights.wait()
        gather.first(functools.partial(mix_back, wv, me, dm_ref))

    @pl.when(step == pl.num_programs(0) - 1)
    def _():
        gather.close(back_ref)
        small.close(small_ref)
        links.finish()


def forward(x, target, z, local_weight, bias, rb, bt, cols, weight, devices):
    chans, slab, width = x.shape
    own = weight.shape[0]
    half = chans * GROUP
    bands = slab // ROWS
    band = pl.BlockSpec((chans, ROWS, width), lambda i: (0, jnp.minimum(i, bands - 1), 0))
    later = pl.BlockSpec((chans, ROWS, width), lambda i: (0, jnp.maximum(i - bands, 0), 0))
    shapes = [
        jax.ShapeDtypeStruct(x.shape, BF16),
        jax.ShapeDtypeStruct((2, 2, chans, QUARTER, LANES), BF16),
        jax.ShapeDtypeStruct((own, chans, LANES), F32),
        jax.ShapeDtypeStruct((chans, LANES), F32),
    ]
    return pl.pallas_call(
        forward_kernel,
        grid=(2 * bands,),
        in_specs=[band, band, whole(z), whole(local_weight), whole(bias), whole(rb), whole(bt), HBM, HBM],
        out_specs=[later] + [held(s.shape) for s in shapes[1:]],
        out_shape=shapes,
        scratch_shapes=[
            pltpu.VMEM(cols.shape[1:], BF16),
            pltpu.VMEM((half, half), BF16),
            pltpu.VMEM((half, half), BF16),
            pltpu.VMEM((chans, slab, width), BF16),
            pltpu.VMEM((chans, slab, 2 * KY), F32),
            pltpu.VMEM((half, half), F32),
            pltpu.VMEM((chans, slab, 2 * KY), BF16),
        ] + exchange_scratch(devices, chans, own, True),
        compiler_params=pltpu.CompilerParams(vmem_limit_bytes=LIMIT, collective_id=1, has_side_effects=True),
        name="forward",
    )(x, target, z, local_weight, bias, rb, bt, cols, weight)


def final_kernel(root, cells_count, part_ref, z_ref, rb_ref, cols_ref, xm_ref, dm_ref, small_ref,
                 out_ref, g_ref, local_ref, bias_ref, cols, e_ref, c_sem):
    step = pl.program_id(0)
    chans, rows, width = part_ref.shape
    slab = e_ref.shape[1]
    tile = 512
    pairs = g_ref.shape[0]
    me = lax.axis_index("space")
    table = pltpu.make_async_copy(cols_ref.at[me], cols, c_sem)

    @pl.when(step == 0)
    def _():
        table.start()
        small = small_ref[...]
        local_ref[...] = small[:, :chans] * (1.0 / cells_count)
        column = small[:, chans : chans + 1] * (root / cells_count)
        eye = lax.broadcasted_iota(jnp.int32, (chans, chans), 0) == lax.broadcasted_iota(jnp.int32, (chans, chans), 1)
        bias_ref[...] = jnp.sum(jnp.where(eye, column, 0.0), axis=0, keepdims=True)
        table.wait()
        expand_rows(z_ref, cols[...], slab, e_ref)

    def one_band(i, carry):
        first = pl.multiple_of(i * BAND, BAND)
        here = pl.ds(first, BAND)
        e = e_ref[:, pl.ds(pl.multiple_of(step * rows + first, BAND), BAND), :]
        e = e.reshape(chans * BAND, LANES)
        for start in range(0, width, tile):
            cells = pl.ds(start, tile)
            part = part_ref[:, here, cells].reshape(chans * BAND, tile).astype(F32)
            out = dot(e, rb_ref[:, cells]) + part
            out_ref[:, here, cells] = out.astype(BF16).reshape(chans, BAND, tile)
        return carry

    lax.fori_loop(0, rows // BAND, one_band, 0)
    for i in range(pairs):
        index = step * pairs + i
        x = xm_ref[pl.ds(index, 1), :]
        re, im = halves(x)
        d = dm_ref[index // chans]
        g_ref[i] = cat(re, re) * d + cat(im, -im) * swap(d)


def final(part, z, rb, cols, own_modes, delta_modes, small, height):
    chans, slab, width = part.shape
    own = own_modes.shape[0]
    steps = slab // LAST_ROWS
    pairs = own * chans // steps
    band = pl.BlockSpec((chans, LAST_ROWS, width), lambda i: (0, i, 0))
    own_modes = own_modes.reshape(own * chans, LANES)
    cells_count = height * width
    return pl.pallas_call(
        functools.partial(final_kernel, math.sqrt(cells_count), cells_count),
        grid=(steps,),
        in_specs=[band, whole(z), whole(rb), HBM, whole(own_modes), whole(delta_modes), whole(small)],
        out_specs=[
            band,
            pl.BlockSpec((pairs, chans, LANES), lambda i: (i, 0, 0)),
            held((chans, chans)),
            held((1, chans)),
        ],
        out_shape=[
            jax.ShapeDtypeStruct(part.shape, BF16),
            jax.ShapeDtypeStruct((own * chans, chans, LANES), F32),
            jax.ShapeDtypeStruct((chans, chans), F32),
            jax.ShapeDtypeStruct((1, chans), F32),
        ],
        scratch_shapes=[
            pltpu.VMEM(cols.shape[1:], BF16),
            pltpu.VMEM((chans, slab, 2 * KY), BF16),
            pltpu.SemaphoreType.DMA,
        ],
        compiler_params=pltpu.CompilerParams(vmem_limit_bytes=LIMIT),
        name="final",
    )(part, z, rb, cols, own_modes, delta_modes, small)


def per_device(inputs, target, spectral_weight, local_weight, bias_term):
    samples, chans, slab, width = inputs.shape
    devices = lax.axis_size("space")
    height = slab * devices

    table = row_table(height, width, mode_order(devices))
    rb = jnp.asarray(table)
    bt = jnp.asarray(np.ascontiguousarray(table.T))
    ones = np.zeros((LANES, width), ml_dtypes.bfloat16)
    ones[:3] = 1.0
    rb_bias = jnp.asarray(np.concatenate([table, ones]))
    cols = jnp.asarray(column_table(height, devices))
    bias = jnp.broadcast_to(bias_term[:, None], (chans, LANES))

    x = inputs.reshape(chans, slab, width)
    z, own_modes = analysis(x, bt, cols, spectral_weight, devices)
    part, z, delta_modes, small = forward(
        x, target.reshape(chans, slab, width), z, local_weight, bias, rb_bias, rb, cols, spectral_weight, devices
    )
    grad_input, grad_spectral, grad_local, grad_bias = final(
        part, z, rb, cols, own_modes, delta_modes, small, height
    )
    return (
        grad_input.reshape(inputs.shape),
        grad_spectral.reshape(spectral_weight.shape),
        grad_local,
        grad_bias.reshape(chans),
    )


def solution(mesh):
    return jax.shard_map(
        per_device,
        mesh=mesh,
        in_specs=(
            P("dom", None, "space", None),
            P("dom", None, "space", None),
            P("space", None, None, None),
            P(),
            P(),
        ),
        out_specs=(
            P("dom", None, "space", None),
            P("space", "dom", None, None),
            P("dom", None),
            P("dom"),
        ),
        check_vma=False,
    )
```

```python
import functools
import math

import jax
import jax.numpy as jnp
import ml_dtypes
import numpy as np
from jax import lax
from jax.experimental import pallas as pl
from jax.experimental.pallas import tpu as pltpu
from jax.sharding import PartitionSpec as P

KX = 64
KY = 64
LANES = 2 * KX
QUARTER = KY // 4
LIMIT = 56 * 1024 * 1024
ROWS = 16
BAND = 16
GROUP = 8
CHUNK = 8
HALF = 16
THIRD = 1
MIX = 4
LAST_ROWS = 32
F32 = jnp.float32
BF16 = jnp.bfloat16
NT = (((1,), (1,)), ((), ()))
dot = functools.partial(jnp.dot, preferred_element_type=F32)
dot_nt = functools.partial(lax.dot_general, dimension_numbers=NT, preferred_element_type=F32)


def mode_order(devices):
    own = KY // devices
    return np.arange(KY).reshape(devices // 4, 2, 2, own).transpose(2, 1, 0, 3).reshape(-1)


def row_table(height, width, order):
    angles = (order[:, None] * np.arange(width)[None, :] % width) * (2.0 * math.pi / width)
    factor = 1.0 / math.sqrt(height * width)
    return np.concatenate([np.cos(angles) * factor, -np.sin(angles) * factor]).astype(ml_dtypes.bfloat16)


def column_table(height, devices):
    column = np.arange(KX)
    frequency = np.where(column < KX // 2, column, column + height - KX)
    angles = (np.arange(height)[:, None] * frequency[None, :] % height) * (2.0 * math.pi / height)
    cosines, sines = np.cos(angles), np.sin(angles)
    parts = np.stack([np.concatenate([cosines, -sines], 1), np.concatenate([sines, cosines], 1)])
    slab = height // devices
    table = parts.reshape(2, devices, slab, LANES).transpose(1, 0, 2, 3).reshape(devices, 2 * slab, LANES)
    table = table.astype(np.float32)
    hi = table.astype(ml_dtypes.bfloat16)
    lo = (table - hi.astype(np.float32)).astype(ml_dtypes.bfloat16)
    return np.concatenate([hi, lo], axis=2)


def halves(value):
    half = value.shape[-1] // 2
    return value[..., :half], value[..., half:]


def cat(a, b):
    return jnp.concatenate([a, b], axis=-1)


def columns_of(row_modes, table):
    parts = []
    for value in row_modes:
        turned = value.T
        parts.append(cat(turned[:KY], turned[KY:]))
    both = jnp.concatenate(parts, axis=0).astype(BF16)
    hi, lo = halves(dot(both, table))
    return hi + lo


def expand_rows(z_ref, table, slab, e_ref):
    chans = z_ref.shape[2]
    left = table[:slab]
    pair = 8

    def body(i, carry):
        parts = []
        for k in range(pair):
            z = z_ref[:, :, i * pair + k].reshape(KY, LANES)
            re, im = halves(z)
            both = jnp.concatenate([z, cat(im, -re)], axis=0)
            parts.append(cat(both, both))
        out = dot_nt(left, jnp.concatenate(parts, axis=0)).astype(BF16)
        for k in range(pair):
            e_ref[i * pair + k] = out[:, k * 2 * KY : (k + 1) * 2 * KY]
        return carry

    lax.fori_loop(0, chans // pair, body, 0)


def place():
    devices = lax.axis_size("space")
    me = lax.axis_index("space")
    return devices // 4, me, lax.rem(me, 2), lax.rem(me // 2, 2), me // 4


def peers():
    nz, me, core, mid, z = place()
    across = me + 1 - 2 * core
    beside = me + 2 - 4 * mid
    along = [lax.rem(z + i, nz) for i in range(nz)]
    return across, beside, along, [a * 4 + mid * 2 + core for a in along]


def greet():
    across, beside, _, line = peers()
    barrier = pltpu.get_barrier_semaphore()
    for target in [across, beside] + line[1:]:
        pl.semaphore_signal(barrier, inc=1, device_id={"space": target}, device_id_type=pl.DeviceIdType.MESH)


def greeted():
    pl.semaphore_wait(pltpu.get_barrier_semaphore(), len(peers()[3]) + 1)


def remote(src, dst, send_sem, recv_sem, target):
    return pltpu.make_async_remote_copy(
        src_ref=src,
        dst_ref=dst,
        send_sem=send_sem,
        recv_sem=recv_sem,
        device_id={"space": target},
        device_id_type=pl.DeviceIdType.MESH,
    )


def exchange_scratch(devices, chans, own, small):
    nz = devices // 4
    parts, wide = chans // CHUNK, chans // HALF
    shapes = [
        pltpu.VMEM((parts, 2, 2, CHUNK, QUARTER, LANES), BF16),
        pltpu.VMEM((parts, 2, CHUNK, QUARTER, LANES), BF16),
        pltpu.VMEM((parts, CHUNK, QUARTER, LANES), BF16),
        pltpu.VMEM((parts, CHUNK, QUARTER, LANES), BF16),
        pltpu.VMEM((parts, CHUNK, QUARTER, LANES), F32),
        pltpu.VMEM((parts, nz, own, CHUNK, LANES), F32),
        pltpu.VMEM((parts, nz, own, CHUNK, LANES), BF16),
        pltpu.VMEM((parts, nz, own, CHUNK, LANES), BF16),
        pltpu.VMEM((wide, nz, own, HALF, LANES), BF16),
        pltpu.VMEM((wide, HALF, QUARTER, LANES), F32),
        pltpu.VMEM((wide, 2, 2, HALF, QUARTER, LANES), BF16),
        pltpu.VMEM((own, chans, chans, LANES), F32),
        pltpu.SemaphoreType.DMA((nz + 1, parts)),
        pltpu.SemaphoreType.DMA((nz + 1, parts)),
        pltpu.SemaphoreType.DMA((nz + 2, wide)),
        pltpu.SemaphoreType.DMA((nz + 2, wide)),
        pltpu.SemaphoreType.DMA,
        pltpu.SemaphoreType.DMA,
    ]
    if small:
        shapes += [
            pltpu.VMEM((4, chans, LANES), F32),
            pltpu.VMEM((nz, chans, LANES), F32),
            pltpu.SemaphoreType.DMA((nz + 1,)),
            pltpu.SemaphoreType.DMA((nz + 1,)),
        ]
    return shapes


class Sums:
    def __init__(self, scratch):
        self.m, self.r1, self.s2, self.r2, self.acc, self.s3f, self.s3, self.r3 = scratch[:8]
        self.send_sem, self.recv_sem = scratch[12:14]
        self.nz, _, self.core, self.mid, self.z = place()
        self.across, self.beside, self.along, self.line = peers()

    def copy(self, stage, c):
        if stage == 0:
            ends = self.m.at[c, 1 - self.core], self.r1.at[c], self.across
        elif stage == 1:
            ends = self.s2.at[c], self.r2.at[c], self.beside
        else:
            i = stage - 1
            ends = self.s3.at[c, self.along[i]], self.r3.at[c, i], self.line[i]
        return remote(ends[0], ends[1], self.send_sem.at[stage, c], self.recv_sem.at[stage, c], ends[2])

    def first(self, c):
        self.copy(0, c).start()

    def second(self, c):
        self.copy(0, c).wait_recv()
        m, r1, core, mid = self.m, self.r1, self.core, self.mid
        self.s2[c] = (m[c, core, 1 - mid].astype(F32) + r1[c, 1 - mid].astype(F32)).astype(BF16)
        self.copy(1, c).start()
        self.acc[c] = m[c, core, mid].astype(F32) + r1[c, mid].astype(F32)

    def third(self, c):
        self.copy(1, c).wait_recv()
        self.acc[c] += self.r2[c].astype(F32)
        own = self.s3.shape[2]
        for a in range(self.nz):
            for k in range(own):
                block = self.acc[c, :, a * own + k, :]
                self.s3f[c, a, k] = block
                self.s3[c, a, k] = block.astype(BF16)
        for i in range(1, self.nz):
            self.copy(1 + i, c).start()

    def advance(self, c):
        self.first(c)
        pl.when(c >= 1)(lambda: self.second(c - 1))
        pl.when(c >= 2)(lambda: self.third(c - 2))

    def close(self, own_ref):
        parts, own = self.m.shape[0], self.s3.shape[2]
        for c in range(parts):
            for i in range(1, self.nz):
                self.copy(1 + i, c).wait_recv()
            for k in range(own):
                total = self.s3f[c, self.z, k]
                for i in range(1, self.nz):
                    total = total + self.r3[c, i, k].astype(F32)
                own_ref[k, c * CHUNK : (c + 1) * CHUNK] = total

    def finish(self):
        for c in range(self.m.shape[0]):
            for stage in range(self.nz + 1):
                self.copy(stage, c).wait_send()


class Small:
    def __init__(self, scratch):
        self.sm, self.rz, self.send_sem, self.recv_sem = scratch[18:22]
        self.nz, _, _, _, self.z = place()
        self.across, self.beside, _, self.line = peers()

    def copy(self, stage):
        if stage == 0:
            ends = self.sm.at[0], self.sm.at[1], self.across
        elif stage == 1:
            ends = self.sm.at[2], self.sm.at[3], self.beside
        else:
            ends = self.rz.at[self.z], self.rz.at[self.z], self.line[stage - 1]
        return remote(ends[0], ends[1], self.send_sem.at[stage], self.recv_sem.at[stage], ends[2])

    def first(self):
        self.copy(0).start()

    def second(self):
        self.copy(0).wait_recv()
        self.sm[2] = self.sm[0] + self.sm[1]
        self.copy(1).start()

    def third(self):
        self.copy(1).wait_recv()
        self.rz[self.z] = self.sm[2] + self.sm[3]
        for i in range(1, self.nz):
            self.copy(1 + i).start()

    def close(self, out_ref):
        for i in range(1, self.nz):
            self.copy(1 + i).wait_recv()
        total = self.rz[0]
        for i in range(1, self.nz):
            total = total + self.rz[i]
        out_ref[...] = total
        for stage in range(self.nz + 1):
            self.copy(stage).wait_send()


class Gather:
    def __init__(self, scratch):
        self.zg, self.turn, self.zt = scratch[8:11]
        self.send_sem, self.recv_sem = scratch[14:16]
        self.nz, _, self.core, self.mid, self.z = place()
        self.across, self.beside, _, self.line = peers()
        self.wide = self.zg.shape[0]

    def copy(self, stage, g):
        if stage == 0:
            src, target = self.zt.at[g, self.core, self.mid], self.beside
        elif stage < self.nz:
            src, target = self.zg.at[g, self.z], self.line[stage]
        elif stage == self.nz:
            src, target = self.zt.at[g, self.core, self.mid], self.across
        else:
            src, target = self.zt.at[g, self.core, 1 - self.mid], self.across
        return remote(src, src, self.send_sem.at[stage, g], self.recv_sem.at[stage, g], target)

    def first(self, mix):
        for g in range(self.wide):
            mix(g, self.zg)
            for i in range(1, self.nz):
                self.copy(i, g).start()

    def close(self, z_ref):
        zg, turn, zt = self.zg, self.turn, self.zt
        own = zg.shape[2]
        for g in range(self.wide):
            for i in range(1, self.nz):
                self.copy(i, g).wait_recv()
            for a in range(self.nz):
                for k in range(own):
                    turn[g, :, a * own + k, :] = zg[g, a, k].astype(F32)
            zt[g, self.core, self.mid] = turn[g].astype(BF16)
            self.copy(0, g).start()
            self.copy(self.nz, g).start()
        for g in range(self.wide):
            self.copy(0, g).wait_recv()
            self.copy(self.nz + 1, g).start()
        for g in range(self.wide):
            self.copy(self.nz, g).wait_recv()
            self.copy(self.nz + 1, g).wait_recv()
            z_ref[:, :, g * HALF : (g + 1) * HALF] = zt[g]
            for stage in range(self.nz + 2):
                self.copy(stage, g).wait_send()


def mode_gain(me, own, k):
    return jnp.where(me * own + k == 0, 1.0, 2.0).astype(F32)


def swap(value):
    a, b = halves(value)
    return cat(b, a)


def mix_forward(w_ref, me, x_ref, g, z_ref):
    own, chans = w_ref.shape[:2]
    _, _, _, _, z = place()
    for k in range(own):
        x = x_ref[k]
        x_sw = swap(x)
        first = jnp.zeros((HALF, LANES), F32)
        second = jnp.zeros((HALF, LANES), F32)
        for c in range(chans):
            w = w_ref[k, c, g * HALF : (g + 1) * HALF]
            first = first + x[c : c + 1] * w
            second = second + x_sw[c : c + 1] * w
        a, b = halves(first)
        c, d = halves(second)
        z_ref[g, z, k] = (cat(a - b, c + d) * mode_gain(me, own, k)).astype(BF16)


def mix_back(w_ref, me, d_ref, g, z_ref):
    own = w_ref.shape[0]
    _, _, _, _, z = place()
    for k in range(own):
        d = d_ref[k]
        d_sw = swap(d)
        firsts, seconds = [], []
        for c in range(g * HALF, (g + 1) * HALF):
            w = w_ref[k, c]
            firsts.append(jnp.sum(d * w, axis=0, keepdims=True))
            seconds.append(jnp.sum(d_sw * w, axis=0, keepdims=True))
        a, b = halves(jnp.concatenate(firsts, axis=0))
        e, f = halves(jnp.concatenate(seconds, axis=0))
        z_ref[g, z, k] = cat(a + b, e - f).astype(BF16)


def analysis_kernel(x_ref, bt_ref, cols_ref, w_ref, z_ref, own_ref, cols, *scratch):
    step = pl.program_id(0)
    count, rows, width = x_ref.shape
    m, wv, w_sem, c_sem = scratch[0], scratch[11], scratch[16], scratch[17]
    me = lax.axis_index("space")
    weights = pltpu.make_async_copy(w_ref, wv, w_sem)
    table = pltpu.make_async_copy(cols_ref.at[me], cols, c_sem)

    @pl.when(step == 0)
    def _():
        greet()
        table.start()
        weights.start()
        table.wait()

    flat = x_ref[...].reshape(count * rows, width)
    row_modes = dot(flat, bt_ref[...])
    modes = columns_of([row_modes[c * rows : (c + 1) * rows] for c in range(count)], cols[...]).astype(BF16)
    for c in range(count):
        m[step, :, :, c] = modes[c * KY : (c + 1) * KY].reshape(2, 2, QUARTER, LANES)

    @pl.when(step == 0)
    def _():
        greeted()

    sums = Sums(scratch)
    sums.advance(step)

    @pl.when(step == pl.num_programs(0) - 1)
    def _():
        sums.second(step)
        sums.third(step - 1)
        sums.third(step)
        sums.close(own_ref)
        weights.wait()
        gather = Gather(scratch)
        gather.first(functools.partial(mix_forward, wv, me, own_ref))
        gather.close(z_ref)
        sums.finish()


def whole(a):
    return pl.BlockSpec(a.shape, lambda i: (0,) * a.ndim)


def held(shape):
    return pl.BlockSpec(shape, lambda i: (0,) * len(shape))


HBM = pl.BlockSpec(memory_space=pl.ANY)


def analysis(x, bt, cols, weight, devices):
    chans, rows, width = x.shape
    own = weight.shape[0]
    block = CHUNK
    shapes = [
        jax.ShapeDtypeStruct((2, 2, chans, QUARTER, LANES), BF16),
        jax.ShapeDtypeStruct((own, chans, LANES), F32),
    ]
    return pl.pallas_call(
        analysis_kernel,
        grid=(chans // block,),
        in_specs=[pl.BlockSpec((block, rows, width), lambda i: (i, 0, 0)), whole(bt), HBM, HBM],
        out_specs=[held(s.shape) for s in shapes],
        out_shape=shapes,
        scratch_shapes=[pltpu.VMEM(cols.shape[1:], BF16)] + exchange_scratch(devices, chans, own, False),
        compiler_params=pltpu.CompilerParams(vmem_limit_bytes=LIMIT, collective_id=0, has_side_effects=True),
        name="analysis",
    )(x, bt, cols, weight)


def spread(weight, flip, scale):
    chans = weight.shape[0]
    flat = chans * GROUP
    chosen = lax.broadcasted_iota(jnp.int32, (flat, chans), 0) // GROUP == lax.broadcasted_iota(jnp.int32, (flat, chans), 1)
    chosen = jnp.where(chosen, 1.0, 0.0).astype(BF16)
    tall = (dot_nt if flip else dot)(chosen, weight).astype(BF16)
    wide = dot_nt(tall, chosen)
    first = lax.broadcasted_iota(jnp.int32, (flat, flat), 0) % GROUP
    second = lax.broadcasted_iota(jnp.int32, (flat, flat), 1) % GROUP
    return jnp.where(first == second, wide * scale, 0.0).astype(BF16)


def groups_of(value):
    chans, rows, last = value.shape
    return [value[:, g : g + GROUP].reshape(chans * GROUP, last) for g in range(0, rows, GROUP)]


def joined(groups, chans):
    return jnp.concatenate([g.reshape(chans, GROUP, g.shape[-1]) for g in groups], axis=1)


def bias_block(bias):
    hi = bias.astype(BF16).astype(F32)
    mid = (bias - hi).astype(BF16).astype(F32)
    lo = bias - hi - mid
    lane = lax.broadcasted_iota(jnp.int32, bias.shape, 1)
    return jnp.where(lane == 0, hi, jnp.where(lane == 1, mid, jnp.where(lane == 2, lo, 0.0))).astype(BF16)


PHI = (1.5954356609777183, 0.29438608777535386, -0.010105857224310238)


def twice_delta(s, target):
    one = lambda value: jnp.asarray(value, BF16)
    q = s * s
    p = jnp.minimum(q, one(9.0))
    p = (one(PHI[2]) * p + one(PHI[1])) * p + one(PHI[0])
    a = one(1.0) + jnp.tanh(s * p)
    e = jnp.exp2(q * one(-2.0 / math.log(2.0)) + one(math.log2(4.0 / math.sqrt(2.0 * math.pi))))
    return (s * a - target) * (a + s * e)


def forward_kernel(x_ref, t_ref, z_ref, lw_ref, bias_ref, rb_ref, bt_ref, cols_ref, w_ref,
                   part_ref, back_ref, dm_ref, small_ref, cols, kron, kron_back, bias_wide, delta_ref, rows_ref, acc_ref, e_ref,
                   *scratch):
    step = pl.program_id(0)
    bands = pl.num_programs(0) // 2
    chans, rows, width = x_ref.shape
    slab = rows_ref.shape[1]
    half = chans * GROUP
    tile = 512
    m, wv, w_sem, c_sem = scratch[0], scratch[11], scratch[16], scratch[17]
    me = lax.axis_index("space")
    weights = pltpu.make_async_copy(w_ref, wv, w_sem)
    table = pltpu.make_async_copy(cols_ref.at[me], cols, c_sem)

    @pl.when(step == 0)
    def _():
        greet()
        table.start()
        weights.start()
        acc_ref[...] = jnp.zeros_like(acc_ref)
        kron[...] = spread(lw_ref[...], True, 0.5)
        kron_back[...] = spread(lw_ref[...], False, 0.5)
        eye = lax.broadcasted_iota(jnp.int32, (half, chans), 0) // GROUP
        eye = eye == lax.broadcasted_iota(jnp.int32, (half, chans), 1)
        column = jnp.sum(jnp.where(eye, bias_ref[...] * 0.5, 0.0), axis=1, keepdims=True)
        bias_wide[...] = bias_block(jnp.broadcast_to(column, (half, LANES)))
        table.wait()
        expand_rows(z_ref, cols[...], slab, e_ref)

    @pl.when(step < bands)
    def _():
        band = pl.ds(pl.multiple_of(step * rows, rows), rows)
        e = (e_ref[:, band, :].astype(F32) * 0.5).astype(BF16)
        left = [cat(group, bias_wide[...]) for group in groups_of(e)]
        deltas = []
        for start in range(0, width, tile):
            cells = pl.ds(start, tile)
            sums = []
            for lhs, x in zip(left, groups_of(x_ref[:, :, cells])):
                sums.append(dot(kron[...], x) + dot(lhs, rb_ref[:, cells]))
            delta = twice_delta(joined(sums, chans).astype(BF16), t_ref[:, :, cells])
            delta_ref[:, band, cells] = delta
            deltas.append(groups_of(delta))
        row_modes = []
        for g, x in enumerate(groups_of(x_ref[...])):
            delta = jnp.concatenate([d[g] for d in deltas], axis=1)
            both = dot_nt(jnp.concatenate([x, bt_ref[...]], axis=0), delta)
            acc_ref[...] += both[:half]
            row_modes.append(both[half:].T)
        rows_ref[:, band, :] = joined(row_modes, chans) * 0.5

    @pl.when(step >= bands)
    def _():
        band = pl.ds(pl.multiple_of((step - bands) * rows, rows), rows)
        for start in range(0, width, tile):
            cells = pl.ds(start, tile)
            out = [dot(kron_back[...], d) for d in groups_of(delta_ref[:, band, cells])]
            part_ref[:, :, cells] = joined(out, chans).astype(BF16)

    small = Small(scratch)
    links = Sums(scratch)
    gather = Gather(scratch)
    own = dm_ref.shape[0]
    chunks = chans // CHUNK

    @pl.when(step == bands - 1)
    def _():
        first = lax.broadcasted_iota(jnp.int32, (half, half), 0) % GROUP
        second = lax.broadcasted_iota(jnp.int32, (half, half), 1) % GROUP
        kept = jnp.where(first == second, acc_ref[...], 0.0)
        kept = jnp.sum(kept.reshape(chans, GROUP, half), axis=1)
        group = lax.broadcasted_iota(jnp.int32, (half, LANES), 0) // GROUP
        lane = lax.broadcasted_iota(jnp.int32, (half, LANES), 1)
        group = jnp.where(group == lane, 0.5, 0.0).astype(BF16)
        hi = kept.astype(BF16)
        rest = kept - hi.astype(F32)
        lo = rest.astype(BF16)
        last = (rest - lo.astype(F32)).astype(BF16)
        terms = dot(hi, group) + (dot(lo, group) + dot(last, group))
        sums = jnp.sum(rows_ref[...], axis=1)[:, :1]
        lane = lax.broadcasted_iota(jnp.int32, (chans, LANES), 1)
        small.sm[0] = jnp.where(lane == chans, sums, terms)
        greeted()
        small.first()

        def body(i, carry):
            modes = columns_of([rows_ref[i * CHUNK + k] for k in range(CHUNK)], cols[...]).astype(BF16)
            for k in range(CHUNK):
                m[i, :, :, k] = modes[k * KY : (k + 1) * KY].reshape(2, 2, QUARTER, LANES)
            links.first(i)
            pl.when(i >= 1)(lambda: links.second(i - 1))
            return carry

        lax.fori_loop(0, chunks, body, 0)
        links.second(chunks - 1)
        small.second()

    @pl.when(step == bands + jnp.minimum(THIRD, bands - 1))
    def _():
        for c in range(chunks):
            links.third(c)
        small.third()

    @pl.when(step == bands + jnp.minimum(MIX, bands - 1))
    def _():
        links.close(dm_ref)
        for k in range(own):
            dm_ref[k] = dm_ref[k] * mode_gain(me, own, k)
        weights.wait()
        gather.first(functools.partial(mix_back, wv, me, dm_ref))

    @pl.when(step == pl.num_programs(0) - 1)
    def _():
        gather.close(back_ref)
        small.close(small_ref)
        links.finish()


def forward(x, target, z, local_weight, bias, rb, bt, cols, weight, devices):
    chans, slab, width = x.shape
    own = weight.shape[0]
    half = chans * GROUP
    bands = slab // ROWS
    band = pl.BlockSpec((chans, ROWS, width), lambda i: (0, jnp.minimum(i, bands - 1), 0))
    later = pl.BlockSpec((chans, ROWS, width), lambda i: (0, jnp.maximum(i - bands, 0), 0))
    shapes = [
        jax.ShapeDtypeStruct(x.shape, BF16),
        jax.ShapeDtypeStruct((2, 2, chans, QUARTER, LANES), BF16),
        jax.ShapeDtypeStruct((own, chans, LANES), F32),
        jax.ShapeDtypeStruct((chans, LANES), F32),
    ]
    return pl.pallas_call(
        forward_kernel,
        grid=(2 * bands,),
        in_specs=[band, band, whole(z), whole(local_weight), whole(bias), whole(rb), whole(bt), HBM, HBM],
        out_specs=[later] + [held(s.shape) for s in shapes[1:]],
        out_shape=shapes,
        scratch_shapes=[
            pltpu.VMEM(cols.shape[1:], BF16),
            pltpu.VMEM((half, half), BF16),
            pltpu.VMEM((half, half), BF16),
            pltpu.VMEM((half, LANES), BF16),
            pltpu.VMEM((chans, slab, width), BF16),
            pltpu.VMEM((chans, slab, 2 * KY), F32),
            pltpu.VMEM((half, half), F32),
            pltpu.VMEM((chans, slab, 2 * KY), BF16),
        ] + exchange_scratch(devices, chans, own, True),
        compiler_params=pltpu.CompilerParams(vmem_limit_bytes=LIMIT, collective_id=1, has_side_effects=True),
        name="forward",
    )(x, target, z, local_weight, bias, rb, bt, cols, weight)


def final_kernel(root, cells_count, part_ref, z_ref, rb_ref, cols_ref, xm_ref, dm_ref, small_ref,
                 out_ref, g_ref, local_ref, bias_ref, cols, e_ref, c_sem):
    step = pl.program_id(0)
    chans, rows, width = part_ref.shape
    slab = e_ref.shape[1]
    tile = 512
    pairs = g_ref.shape[0]
    me = lax.axis_index("space")
    table = pltpu.make_async_copy(cols_ref.at[me], cols, c_sem)

    @pl.when(step == 0)
    def _():
        table.start()
        small = small_ref[...]
        local_ref[...] = small[:, :chans] * (1.0 / cells_count)
        column = small[:, chans : chans + 1] * (root / cells_count)
        eye = lax.broadcasted_iota(jnp.int32, (chans, chans), 0) == lax.broadcasted_iota(jnp.int32, (chans, chans), 1)
        bias_ref[...] = jnp.sum(jnp.where(eye, column, 0.0), axis=0, keepdims=True)
        table.wait()
        expand_rows(z_ref, cols[...], slab, e_ref)

    def one_band(i, carry):
        first = pl.multiple_of(i * BAND, BAND)
        here = pl.ds(first, BAND)
        e = e_ref[:, pl.ds(pl.multiple_of(step * rows + first, BAND), BAND), :]
        e = e.reshape(chans * BAND, LANES)
        for start in range(0, width, tile):
            cells = pl.ds(start, tile)
            part = part_ref[:, here, cells].reshape(chans * BAND, tile).astype(F32)
            out = dot(e, rb_ref[:, cells]) + part
            out_ref[:, here, cells] = out.astype(BF16).reshape(chans, BAND, tile)
        return carry

    lax.fori_loop(0, rows // BAND, one_band, 0)
    for i in range(pairs):
        index = step * pairs + i
        x = xm_ref[pl.ds(index, 1), :]
        re, im = halves(x)
        d = dm_ref[index // chans]
        g_ref[i] = cat(re, re) * d + cat(im, -im) * swap(d)


def final(part, z, rb, cols, own_modes, delta_modes, small, height):
    chans, slab, width = part.shape
    own = own_modes.shape[0]
    steps = slab // LAST_ROWS
    pairs = own * chans // steps
    band = pl.BlockSpec((chans, LAST_ROWS, width), lambda i: (0, i, 0))
    own_modes = own_modes.reshape(own * chans, LANES)
    cells_count = height * width
    return pl.pallas_call(
        functools.partial(final_kernel, math.sqrt(cells_count), cells_count),
        grid=(steps,),
        in_specs=[band, whole(z), whole(rb), HBM, whole(own_modes), whole(delta_modes), whole(small)],
        out_specs=[
            band,
            pl.BlockSpec((pairs, chans, LANES), lambda i: (i, 0, 0)),
            held((chans, chans)),
            held((1, chans)),
        ],
        out_shape=[
            jax.ShapeDtypeStruct(part.shape, BF16),
            jax.ShapeDtypeStruct((own * chans, chans, LANES), F32),
            jax.ShapeDtypeStruct((chans, chans), F32),
            jax.ShapeDtypeStruct((1, chans), F32),
        ],
        scratch_shapes=[
            pltpu.VMEM(cols.shape[1:], BF16),
            pltpu.VMEM((chans, slab, 2 * KY), BF16),
            pltpu.SemaphoreType.DMA,
        ],
        compiler_params=pltpu.CompilerParams(vmem_limit_bytes=LIMIT),
        name="final",
    )(part, z, rb, cols, own_modes, delta_modes, small)


def per_device(inputs, target, spectral_weight, local_weight, bias_term):
    samples, chans, slab, width = inputs.shape
    devices = lax.axis_size("space")
    height = slab * devices

    table = row_table(height, width, mode_order(devices))
    rb = jnp.asarray(table)
    bt = jnp.asarray(np.ascontiguousarray(table.T))
    ones = np.zeros((LANES, width), ml_dtypes.bfloat16)
    ones[:3] = 1.0
    rb_bias = jnp.asarray(np.concatenate([table, ones]))
    cols = jnp.asarray(column_table(height, devices))
    bias = bias_term.reshape(1, chans)

    x = inputs.reshape(chans, slab, width)
    z, own_modes = analysis(x, bt, cols, spectral_weight, devices)
    part, z, delta_modes, small = forward(
        x, target.reshape(chans, slab, width), z, local_weight, bias, rb_bias, rb, cols, spectral_weight, devices
    )
    grad_input, grad_spectral, grad_local, grad_bias = final(
        part, z, rb, cols, own_modes, delta_modes, small, height
    )
    return (
        grad_input.reshape(inputs.shape),
        grad_spectral.reshape(spectral_weight.shape),
        grad_local,
        grad_bias.reshape(chans),
    )


def solution(mesh):
    return jax.shard_map(
        per_device,
        mesh=mesh,
        in_specs=(
            P("dom", None, "space", None),
            P("dom", None, "space", None),
            P("space", None, None, None),
            P(),
            P(),
        ),
        out_specs=(
            P("dom", None, "space", None),
            P("space", "dom", None, None),
            P("dom", None),
            P("dom"),
        ),
        check_vma=False,
    )
```

```python
import functools
import math

import jax
import jax.numpy as jnp
import ml_dtypes
import numpy as np
from jax import lax
from jax.experimental import pallas as pl
from jax.experimental.pallas import tpu as pltpu
from jax.sharding import PartitionSpec as P

KX = 64
KY = 64
LANES = 2 * KX
QUARTER = KY // 4
LIMIT = 56 * 1024 * 1024
ROWS = 16
BAND = 16
GROUP = 8
CHUNK = 8
HALF = 16
THIRD = 1
MIX = 4
LAST_ROWS = 32
F32 = jnp.float32
BF16 = jnp.bfloat16
NT = (((1,), (1,)), ((), ()))
dot = functools.partial(jnp.dot, preferred_element_type=F32)
dot_nt = functools.partial(lax.dot_general, dimension_numbers=NT, preferred_element_type=F32)


def mode_order(devices):
    own = KY // devices
    return np.arange(KY).reshape(devices // 4, 2, 2, own).transpose(2, 1, 0, 3).reshape(-1)


def row_table(height, width, order):
    angles = (order[:, None] * np.arange(width)[None, :] % width) * (2.0 * math.pi / width)
    factor = 1.0 / math.sqrt(height * width)
    return np.concatenate([np.cos(angles) * factor, -np.sin(angles) * factor]).astype(ml_dtypes.bfloat16)


def column_table(height, devices):
    column = np.arange(KX)
    frequency = np.where(column < KX // 2, column, column + height - KX)
    angles = (np.arange(height)[:, None] * frequency[None, :] % height) * (2.0 * math.pi / height)
    cosines, sines = np.cos(angles), np.sin(angles)
    parts = np.stack([np.concatenate([cosines, -sines], 1), np.concatenate([sines, cosines], 1)])
    slab = height // devices
    table = parts.reshape(2, devices, slab, LANES).transpose(1, 0, 2, 3).reshape(devices, 2 * slab, LANES)
    table = table.astype(np.float32)
    hi = table.astype(ml_dtypes.bfloat16)
    lo = (table - hi.astype(np.float32)).astype(ml_dtypes.bfloat16)
    return np.concatenate([hi, lo], axis=2)


def halves(value):
    half = value.shape[-1] // 2
    return value[..., :half], value[..., half:]


def cat(a, b):
    return jnp.concatenate([a, b], axis=-1)


def columns_of(row_modes, table):
    parts = []
    for value in row_modes:
        turned = value.T
        parts.append(cat(turned[:KY], turned[KY:]))
    both = jnp.concatenate(parts, axis=0).astype(BF16)
    hi, lo = halves(dot(both, table))
    return hi + lo


def expand_rows(z_ref, table, slab, e_ref):
    chans = z_ref.shape[2]
    left = table[:slab]
    pair = 32

    def body(i, carry):
        parts = []
        for k in range(pair):
            z = z_ref[:, :, i * pair + k].reshape(KY, LANES)
            re, im = halves(z)
            both = jnp.concatenate([z, cat(im, -re)], axis=0)
            parts.append(cat(both, both))
        out = dot_nt(left, jnp.concatenate(parts, axis=0)).astype(BF16)
        for k in range(pair):
            e_ref[i * pair + k] = out[:, k * 2 * KY : (k + 1) * 2 * KY]
        return carry

    lax.fori_loop(0, chans // pair, body, 0)


def place():
    devices = lax.axis_size("space")
    me = lax.axis_index("space")
    return devices // 4, me, lax.rem(me, 2), lax.rem(me // 2, 2), me // 4


def peers():
    nz, me, core, mid, z = place()
    across = me + 1 - 2 * core
    beside = me + 2 - 4 * mid
    along = [lax.rem(z + i, nz) for i in range(nz)]
    return across, beside, along, [a * 4 + mid * 2 + core for a in along]


def greet():
    across, beside, _, line = peers()
    barrier = pltpu.get_barrier_semaphore()
    for target in [across, beside] + line[1:]:
        pl.semaphore_signal(barrier, inc=1, device_id={"space": target}, device_id_type=pl.DeviceIdType.MESH)


def greeted():
    pl.semaphore_wait(pltpu.get_barrier_semaphore(), len(peers()[3]) + 1)


def remote(src, dst, send_sem, recv_sem, target):
    return pltpu.make_async_remote_copy(
        src_ref=src,
        dst_ref=dst,
        send_sem=send_sem,
        recv_sem=recv_sem,
        device_id={"space": target},
        device_id_type=pl.DeviceIdType.MESH,
    )


def exchange_scratch(devices, chans, own, small):
    nz = devices // 4
    parts, wide = chans // CHUNK, chans // HALF
    shapes = [
        pltpu.VMEM((parts, 2, 2, CHUNK, QUARTER, LANES), BF16),
        pltpu.VMEM((parts, 2, CHUNK, QUARTER, LANES), BF16),
        pltpu.VMEM((parts, CHUNK, QUARTER, LANES), BF16),
        pltpu.VMEM((parts, CHUNK, QUARTER, LANES), BF16),
        pltpu.VMEM((parts, CHUNK, QUARTER, LANES), F32),
        pltpu.VMEM((parts, nz, own, CHUNK, LANES), F32),
        pltpu.VMEM((parts, nz, own, CHUNK, LANES), BF16),
        pltpu.VMEM((parts, nz, own, CHUNK, LANES), BF16),
        pltpu.VMEM((wide, nz, own, HALF, LANES), BF16),
        pltpu.VMEM((wide, HALF, QUARTER, LANES), F32),
        pltpu.VMEM((wide, 2, 2, HALF, QUARTER, LANES), BF16),
        pltpu.VMEM((own, chans, chans, LANES), F32),
        pltpu.SemaphoreType.DMA((nz + 1, parts)),
        pltpu.SemaphoreType.DMA((nz + 1, parts)),
        pltpu.SemaphoreType.DMA((nz + 2, wide)),
        pltpu.SemaphoreType.DMA((nz + 2, wide)),
        pltpu.SemaphoreType.DMA,
        pltpu.SemaphoreType.DMA,
    ]
    if small:
        shapes += [
            pltpu.VMEM((4, chans, LANES), F32),
            pltpu.VMEM((nz, chans, LANES), F32),
            pltpu.SemaphoreType.DMA((nz + 1,)),
            pltpu.SemaphoreType.DMA((nz + 1,)),
        ]
    return shapes


class Sums:
    def __init__(self, scratch):
        self.m, self.r1, self.s2, self.r2, self.acc, self.s3f, self.s3, self.r3 = scratch[:8]
        self.send_sem, self.recv_sem = scratch[12:14]
        self.nz, _, self.core, self.mid, self.z = place()
        self.across, self.beside, self.along, self.line = peers()

    def copy(self, stage, c):
        if stage == 0:
            ends = self.m.at[c, 1 - self.core], self.r1.at[c], self.across
        elif stage == 1:
            ends = self.s2.at[c], self.r2.at[c], self.beside
        else:
            i = stage - 1
            ends = self.s3.at[c, self.along[i]], self.r3.at[c, i], self.line[i]
        return remote(ends[0], ends[1], self.send_sem.at[stage, c], self.recv_sem.at[stage, c], ends[2])

    def first(self, c):
        self.copy(0, c).start()

    def second(self, c):
        self.copy(0, c).wait_recv()
        m, r1, core, mid = self.m, self.r1, self.core, self.mid
        self.s2[c] = (m[c, core, 1 - mid].astype(F32) + r1[c, 1 - mid].astype(F32)).astype(BF16)
        self.copy(1, c).start()
        self.acc[c] = m[c, core, mid].astype(F32) + r1[c, mid].astype(F32)

    def third(self, c):
        self.copy(1, c).wait_recv()
        self.acc[c] += self.r2[c].astype(F32)
        own = self.s3.shape[2]
        for a in range(self.nz):
            for k in range(own):
                block = self.acc[c, :, a * own + k, :]
                self.s3f[c, a, k] = block
                self.s3[c, a, k] = block.astype(BF16)
        for i in range(1, self.nz):
            self.copy(1 + i, c).start()

    def advance(self, c):
        self.first(c)
        pl.when(c >= 1)(lambda: self.second(c - 1))
        pl.when(c >= 2)(lambda: self.third(c - 2))

    def close(self, own_ref):
        parts, own = self.m.shape[0], self.s3.shape[2]
        for c in range(parts):
            for i in range(1, self.nz):
                self.copy(1 + i, c).wait_recv()
            for k in range(own):
                total = self.s3f[c, self.z, k]
                for i in range(1, self.nz):
                    total = total + self.r3[c, i, k].astype(F32)
                own_ref[k, c * CHUNK : (c + 1) * CHUNK] = total

    def finish(self):
        for c in range(self.m.shape[0]):
            for stage in range(self.nz + 1):
                self.copy(stage, c).wait_send()


class Small:
    def __init__(self, scratch):
        self.sm, self.rz, self.send_sem, self.recv_sem = scratch[18:22]
        self.nz, _, _, _, self.z = place()
        self.across, self.beside, _, self.line = peers()

    def copy(self, stage):
        if stage == 0:
            ends = self.sm.at[0], self.sm.at[1], self.across
        elif stage == 1:
            ends = self.sm.at[2], self.sm.at[3], self.beside
        else:
            ends = self.rz.at[self.z], self.rz.at[self.z], self.line[stage - 1]
        return remote(ends[0], ends[1], self.send_sem.at[stage], self.recv_sem.at[stage], ends[2])

    def first(self):
        self.copy(0).start()

    def second(self):
        self.copy(0).wait_recv()
        self.sm[2] = self.sm[0] + self.sm[1]
        self.copy(1).start()

    def third(self):
        self.copy(1).wait_recv()
        self.rz[self.z] = self.sm[2] + self.sm[3]
        for i in range(1, self.nz):
            self.copy(1 + i).start()

    def close(self, out_ref):
        for i in range(1, self.nz):
            self.copy(1 + i).wait_recv()
        total = self.rz[0]
        for i in range(1, self.nz):
            total = total + self.rz[i]
        out_ref[...] = total
        for stage in range(self.nz + 1):
            self.copy(stage).wait_send()


class Gather:
    def __init__(self, scratch):
        self.zg, self.turn, self.zt = scratch[8:11]
        self.send_sem, self.recv_sem = scratch[14:16]
        self.nz, _, self.core, self.mid, self.z = place()
        self.across, self.beside, _, self.line = peers()
        self.wide = self.zg.shape[0]

    def copy(self, stage, g):
        if stage == 0:
            src, target = self.zt.at[g, self.core, self.mid], self.beside
        elif stage < self.nz:
            src, target = self.zg.at[g, self.z], self.line[stage]
        elif stage == self.nz:
            src, target = self.zt.at[g, self.core, self.mid], self.across
        else:
            src, target = self.zt.at[g, self.core, 1 - self.mid], self.across
        return remote(src, src, self.send_sem.at[stage, g], self.recv_sem.at[stage, g], target)

    def first(self, mix):
        for g in range(self.wide):
            mix(g, self.zg)
            for i in range(1, self.nz):
                self.copy(i, g).start()

    def close(self, z_ref):
        zg, turn, zt = self.zg, self.turn, self.zt
        own = zg.shape[2]
        for g in range(self.wide):
            for i in range(1, self.nz):
                self.copy(i, g).wait_recv()
            for a in range(self.nz):
                for k in range(own):
                    turn[g, :, a * own + k, :] = zg[g, a, k].astype(F32)
            zt[g, self.core, self.mid] = turn[g].astype(BF16)
            self.copy(0, g).start()
            self.copy(self.nz, g).start()
        for g in range(self.wide):
            self.copy(0, g).wait_recv()
            self.copy(self.nz + 1, g).start()
        for g in range(self.wide):
            self.copy(self.nz, g).wait_recv()
            self.copy(self.nz + 1, g).wait_recv()
            z_ref[:, :, g * HALF : (g + 1) * HALF] = zt[g]
            for stage in range(self.nz + 2):
                self.copy(stage, g).wait_send()


def mode_gain(me, own, k):
    return jnp.where(me * own + k == 0, 1.0, 2.0).astype(F32)


def swap(value):
    a, b = halves(value)
    return cat(b, a)


def mix_forward(w_ref, me, x_ref, g, z_ref):
    own, chans = w_ref.shape[:2]
    _, _, _, _, z = place()
    for k in range(own):
        x = x_ref[k]
        x_sw = swap(x)
        first = jnp.zeros((HALF, LANES), F32)
        second = jnp.zeros((HALF, LANES), F32)
        for c in range(chans):
            w = w_ref[k, c, g * HALF : (g + 1) * HALF]
            first = first + x[c : c + 1] * w
            second = second + x_sw[c : c + 1] * w
        a, b = halves(first)
        c, d = halves(second)
        z_ref[g, z, k] = (cat(a - b, c + d) * mode_gain(me, own, k)).astype(BF16)


def mix_back(w_ref, me, d_ref, g, z_ref):
    own = w_ref.shape[0]
    _, _, _, _, z = place()
    for k in range(own):
        d = d_ref[k]
        d_sw = swap(d)
        firsts, seconds = [], []
        for c in range(g * HALF, (g + 1) * HALF):
            w = w_ref[k, c]
            firsts.append(jnp.sum(d * w, axis=0, keepdims=True))
            seconds.append(jnp.sum(d_sw * w, axis=0, keepdims=True))
        a, b = halves(jnp.concatenate(firsts, axis=0))
        e, f = halves(jnp.concatenate(seconds, axis=0))
        z_ref[g, z, k] = cat(a + b, e - f).astype(BF16)


def analysis_kernel(x_ref, bt_ref, cols_ref, w_ref, z_ref, own_ref, cols, *scratch):
    step = pl.program_id(0)
    count, rows, width = x_ref.shape
    m, wv, w_sem, c_sem = scratch[0], scratch[11], scratch[16], scratch[17]
    me = lax.axis_index("space")
    weights = pltpu.make_async_copy(w_ref, wv, w_sem)
    table = pltpu.make_async_copy(cols_ref.at[me], cols, c_sem)

    @pl.when(step == 0)
    def _():
        greet()
        table.start()
        weights.start()
        table.wait()

    flat = x_ref[...].reshape(count * rows, width)
    row_modes = dot(flat, bt_ref[...])
    modes = columns_of([row_modes[c * rows : (c + 1) * rows] for c in range(count)], cols[...]).astype(BF16)
    for c in range(count):
        m[step, :, :, c] = modes[c * KY : (c + 1) * KY].reshape(2, 2, QUARTER, LANES)

    @pl.when(step == 0)
    def _():
        greeted()

    sums = Sums(scratch)
    sums.advance(step)

    @pl.when(step == pl.num_programs(0) - 1)
    def _():
        sums.second(step)
        sums.third(step - 1)
        sums.third(step)
        sums.close(own_ref)
        weights.wait()
        gather = Gather(scratch)
        gather.first(functools.partial(mix_forward, wv, me, own_ref))
        gather.close(z_ref)
        sums.finish()


def whole(a):
    return pl.BlockSpec(a.shape, lambda i: (0,) * a.ndim)


def held(shape):
    return pl.BlockSpec(shape, lambda i: (0,) * len(shape))


HBM = pl.BlockSpec(memory_space=pl.ANY)


def analysis(x, bt, cols, weight, devices):
    chans, rows, width = x.shape
    own = weight.shape[0]
    block = CHUNK
    shapes = [
        jax.ShapeDtypeStruct((2, 2, chans, QUARTER, LANES), BF16),
        jax.ShapeDtypeStruct((own, chans, LANES), F32),
    ]
    return pl.pallas_call(
        analysis_kernel,
        grid=(chans // block,),
        in_specs=[pl.BlockSpec((block, rows, width), lambda i: (i, 0, 0)), whole(bt), HBM, HBM],
        out_specs=[held(s.shape) for s in shapes],
        out_shape=shapes,
        scratch_shapes=[pltpu.VMEM(cols.shape[1:], BF16)] + exchange_scratch(devices, chans, own, False),
        compiler_params=pltpu.CompilerParams(vmem_limit_bytes=LIMIT, collective_id=0, has_side_effects=True),
        name="analysis",
    )(x, bt, cols, weight)


def spread(weight, flip, scale):
    chans = weight.shape[0]
    flat = chans * GROUP
    chosen = lax.broadcasted_iota(jnp.int32, (flat, chans), 0) // GROUP == lax.broadcasted_iota(jnp.int32, (flat, chans), 1)
    chosen = jnp.where(chosen, 1.0, 0.0).astype(BF16)
    tall = (dot_nt if flip else dot)(chosen, weight).astype(BF16)
    wide = dot_nt(tall, chosen)
    first = lax.broadcasted_iota(jnp.int32, (flat, flat), 0) % GROUP
    second = lax.broadcasted_iota(jnp.int32, (flat, flat), 1) % GROUP
    return jnp.where(first == second, wide * scale, 0.0).astype(BF16)


def groups_of(value):
    chans, rows, last = value.shape
    return [value[:, g : g + GROUP].reshape(chans * GROUP, last) for g in range(0, rows, GROUP)]


def joined(groups, chans):
    return jnp.concatenate([g.reshape(chans, GROUP, g.shape[-1]) for g in groups], axis=1)


def bias_block(bias):
    hi = bias.astype(BF16).astype(F32)
    mid = (bias - hi).astype(BF16).astype(F32)
    lo = bias - hi - mid
    lane = lax.broadcasted_iota(jnp.int32, bias.shape, 1)
    return jnp.where(lane == 0, hi, jnp.where(lane == 1, mid, jnp.where(lane == 2, lo, 0.0))).astype(BF16)


PHI = (1.5954356609777183, 0.29438608777535386, -0.010105857224310238)


def twice_delta(s, target):
    one = lambda value: jnp.asarray(value, BF16)
    q = s * s
    p = jnp.minimum(q, one(9.0))
    p = (one(PHI[2]) * p + one(PHI[1])) * p + one(PHI[0])
    a = one(1.0) + jnp.tanh(s * p)
    e = jnp.exp2(q * one(-2.0 / math.log(2.0)) + one(math.log2(4.0 / math.sqrt(2.0 * math.pi))))
    return (s * a - target) * (a + s * e)


def forward_kernel(x_ref, t_ref, z_ref, lw_ref, bias_ref, rb_ref, bt_ref, cols_ref, w_ref,
                   part_ref, back_ref, dm_ref, small_ref, cols, kron, kron_back, bias_wide, delta_ref, rows_ref, acc_ref, e_ref,
                   *scratch):
    step = pl.program_id(0)
    bands = pl.num_programs(0) // 2
    chans, rows, width = x_ref.shape
    slab = rows_ref.shape[1]
    half = chans * GROUP
    tile = 512
    m, wv, w_sem, c_sem = scratch[0], scratch[11], scratch[16], scratch[17]
    me = lax.axis_index("space")
    weights = pltpu.make_async_copy(w_ref, wv, w_sem)
    table = pltpu.make_async_copy(cols_ref.at[me], cols, c_sem)

    @pl.when(step == 0)
    def _():
        greet()
        table.start()
        weights.start()
        acc_ref[...] = jnp.zeros_like(acc_ref)
        kron[...] = spread(lw_ref[...], True, 0.5)
        kron_back[...] = spread(lw_ref[...], False, 0.5)
        eye = lax.broadcasted_iota(jnp.int32, (half, chans), 0) // GROUP
        eye = eye == lax.broadcasted_iota(jnp.int32, (half, chans), 1)
        column = jnp.sum(jnp.where(eye, bias_ref[...] * 0.5, 0.0), axis=1, keepdims=True)
        bias_wide[...] = bias_block(jnp.broadcast_to(column, (half, LANES)))
        table.wait()
        expand_rows(z_ref, cols[...], slab, e_ref)

    @pl.when(step < bands)
    def _():
        band = pl.ds(pl.multiple_of(step * rows, rows), rows)
        e = (e_ref[:, band, :].astype(F32) * 0.5).astype(BF16)
        left = [cat(group, bias_wide[...]) for group in groups_of(e)]
        deltas = []
        for start in range(0, width, tile):
            cells = pl.ds(start, tile)
            sums = []
            for lhs, x in zip(left, groups_of(x_ref[:, :, cells])):
                sums.append(dot(kron[...], x) + dot(lhs, rb_ref[:, cells]))
            delta = twice_delta(joined(sums, chans).astype(BF16), t_ref[:, :, cells])
            delta_ref[:, band, cells] = delta
            deltas.append(groups_of(delta))
        row_modes = []
        for g, x in enumerate(groups_of(x_ref[...])):
            delta = jnp.concatenate([d[g] for d in deltas], axis=1)
            both = dot_nt(jnp.concatenate([x, bt_ref[...]], axis=0), delta)
            acc_ref[...] += both[:half]
            row_modes.append(both[half:].T)
        rows_ref[:, band, :] = joined(row_modes, chans) * 0.5

    @pl.when(step >= bands)
    def _():
        band = pl.ds(pl.multiple_of((step - bands) * rows, rows), rows)
        for start in range(0, width, tile):
            cells = pl.ds(start, tile)
            out = [dot(kron_back[...], d) for d in groups_of(delta_ref[:, band, cells])]
            part_ref[:, :, cells] = joined(out, chans).astype(BF16)

    small = Small(scratch)
    links = Sums(scratch)
    gather = Gather(scratch)
    own = dm_ref.shape[0]
    chunks = chans // CHUNK

    @pl.when(step == bands - 1)
    def _():
        first = lax.broadcasted_iota(jnp.int32, (half, half), 0) % GROUP
        second = lax.broadcasted_iota(jnp.int32, (half, half), 1) % GROUP
        kept = jnp.where(first == second, acc_ref[...], 0.0)
        kept = jnp.sum(kept.reshape(chans, GROUP, half), axis=1)
        group = lax.broadcasted_iota(jnp.int32, (half, LANES), 0) // GROUP
        lane = lax.broadcasted_iota(jnp.int32, (half, LANES), 1)
        group = jnp.where(group == lane, 0.5, 0.0).astype(BF16)
        hi = kept.astype(BF16)
        rest = kept - hi.astype(F32)
        lo = rest.astype(BF16)
        last = (rest - lo.astype(F32)).astype(BF16)
        terms = dot(hi, group) + (dot(lo, group) + dot(last, group))
        sums = jnp.sum(rows_ref[...], axis=1)[:, :1]
        lane = lax.broadcasted_iota(jnp.int32, (chans, LANES), 1)
        small.sm[0] = jnp.where(lane == chans, sums, terms)
        greeted()
        small.first()

        def body(i, carry):
            modes = columns_of([rows_ref[i * CHUNK + k] for k in range(CHUNK)], cols[...]).astype(BF16)
            for k in range(CHUNK):
                m[i, :, :, k] = modes[k * KY : (k + 1) * KY].reshape(2, 2, QUARTER, LANES)
            links.first(i)
            pl.when(i >= 1)(lambda: links.second(i - 1))
            return carry

        lax.fori_loop(0, chunks, body, 0)
        links.second(chunks - 1)
        small.second()

    @pl.when(step == bands + jnp.minimum(THIRD, bands - 1))
    def _():
        for c in range(chunks):
            links.third(c)
        small.third()

    @pl.when(step == bands + jnp.minimum(MIX, bands - 1))
    def _():
        links.close(dm_ref)
        for k in range(own):
            dm_ref[k] = dm_ref[k] * mode_gain(me, own, k)
        weights.wait()
        gather.first(functools.partial(mix_back, wv, me, dm_ref))

    @pl.when(step == pl.num_programs(0) - 1)
    def _():
        gather.close(back_ref)
        small.close(small_ref)
        links.finish()


def forward(x, target, z, local_weight, bias, rb, bt, cols, weight, devices):
    chans, slab, width = x.shape
    own = weight.shape[0]
    half = chans * GROUP
    bands = slab // ROWS
    band = pl.BlockSpec((chans, ROWS, width), lambda i: (0, jnp.minimum(i, bands - 1), 0))
    later = pl.BlockSpec((chans, ROWS, width), lambda i: (0, jnp.maximum(i - bands, 0), 0))
    shapes = [
        jax.ShapeDtypeStruct(x.shape, BF16),
        jax.ShapeDtypeStruct((2, 2, chans, QUARTER, LANES), BF16),
        jax.ShapeDtypeStruct((own, chans, LANES), F32),
        jax.ShapeDtypeStruct((chans, LANES), F32),
    ]
    return pl.pallas_call(
        forward_kernel,
        grid=(2 * bands,),
        in_specs=[band, band, whole(z), whole(local_weight), whole(bias), whole(rb), whole(bt), HBM, HBM],
        out_specs=[later] + [held(s.shape) for s in shapes[1:]],
        out_shape=shapes,
        scratch_shapes=[
            pltpu.VMEM(cols.shape[1:], BF16),
            pltpu.VMEM((half, half), BF16),
            pltpu.VMEM((half, half), BF16),
            pltpu.VMEM((half, LANES), BF16),
            pltpu.VMEM((chans, slab, width), BF16),
            pltpu.VMEM((chans, slab, 2 * KY), F32),
            pltpu.VMEM((half, half), F32),
            pltpu.VMEM((chans, slab, 2 * KY), BF16),
        ] + exchange_scratch(devices, chans, own, True),
        compiler_params=pltpu.CompilerParams(vmem_limit_bytes=LIMIT, collective_id=1, has_side_effects=True),
        name="forward",
    )(x, target, z, local_weight, bias, rb, bt, cols, weight)


def final_kernel(root, cells_count, part_ref, z_ref, rb_ref, cols_ref, xm_ref, dm_ref, small_ref,
                 out_ref, g_ref, local_ref, bias_ref, cols, e_ref, c_sem):
    step = pl.program_id(0)
    chans, rows, width = part_ref.shape
    slab = e_ref.shape[1]
    tile = 512
    pairs = g_ref.shape[0]
    me = lax.axis_index("space")
    table = pltpu.make_async_copy(cols_ref.at[me], cols, c_sem)

    @pl.when(step == 0)
    def _():
        table.start()
        small = small_ref[...]
        local_ref[...] = small[:, :chans] * (1.0 / cells_count)
        column = small[:, chans : chans + 1] * (root / cells_count)
        eye = lax.broadcasted_iota(jnp.int32, (chans, chans), 0) == lax.broadcasted_iota(jnp.int32, (chans, chans), 1)
        bias_ref[...] = jnp.sum(jnp.where(eye, column, 0.0), axis=0, keepdims=True)
        table.wait()
        expand_rows(z_ref, cols[...], slab, e_ref)

    def one_band(i, carry):
        first = pl.multiple_of(i * BAND, BAND)
        here = pl.ds(first, BAND)
        e = e_ref[:, pl.ds(pl.multiple_of(step * rows + first, BAND), BAND), :]
        e = e.reshape(chans * BAND, LANES)
        for start in range(0, width, tile):
            cells = pl.ds(start, tile)
            part = part_ref[:, here, cells].reshape(chans * BAND, tile).astype(F32)
            out = dot(e, rb_ref[:, cells]) + part
            out_ref[:, here, cells] = out.astype(BF16).reshape(chans, BAND, tile)
        return carry

    lax.fori_loop(0, rows // BAND, one_band, 0)
    for i in range(pairs):
        index = step * pairs + i
        x = xm_ref[pl.ds(index, 1), :]
        re, im = halves(x)
        d = dm_ref[index // chans]
        g_ref[i] = cat(re, re) * d + cat(im, -im) * swap(d)


def final(part, z, rb, cols, own_modes, delta_modes, small, height):
    chans, slab, width = part.shape
    own = own_modes.shape[0]
    steps = slab // LAST_ROWS
    pairs = own * chans // steps
    band = pl.BlockSpec((chans, LAST_ROWS, width), lambda i: (0, i, 0))
    own_modes = own_modes.reshape(own * chans, LANES)
    cells_count = height * width
    return pl.pallas_call(
        functools.partial(final_kernel, math.sqrt(cells_count), cells_count),
        grid=(steps,),
        in_specs=[band, whole(z), whole(rb), HBM, whole(own_modes), whole(delta_modes), whole(small)],
        out_specs=[
            band,
            pl.BlockSpec((pairs, chans, LANES), lambda i: (i, 0, 0)),
            held((chans, chans)),
            held((1, chans)),
        ],
        out_shape=[
            jax.ShapeDtypeStruct(part.shape, BF16),
            jax.ShapeDtypeStruct((own * chans, chans, LANES), F32),
            jax.ShapeDtypeStruct((chans, chans), F32),
            jax.ShapeDtypeStruct((1, chans), F32),
        ],
        scratch_shapes=[
            pltpu.VMEM(cols.shape[1:], BF16),
            pltpu.VMEM((chans, slab, 2 * KY), BF16),
            pltpu.SemaphoreType.DMA,
        ],
        compiler_params=pltpu.CompilerParams(vmem_limit_bytes=LIMIT),
        name="final",
    )(part, z, rb, cols, own_modes, delta_modes, small)


def per_device(inputs, target, spectral_weight, local_weight, bias_term):
    samples, chans, slab, width = inputs.shape
    devices = lax.axis_size("space")
    height = slab * devices

    table = row_table(height, width, mode_order(devices))
    rb = jnp.asarray(table)
    bt = jnp.asarray(np.ascontiguousarray(table.T))
    ones = np.zeros((LANES, width), ml_dtypes.bfloat16)
    ones[:3] = 1.0
    rb_bias = jnp.asarray(np.concatenate([table, ones]))
    cols = jnp.asarray(column_table(height, devices))
    bias = bias_term.reshape(1, chans)

    x = inputs.reshape(chans, slab, width)
    z, own_modes = analysis(x, bt, cols, spectral_weight, devices)
    part, z, delta_modes, small = forward(
        x, target.reshape(chans, slab, width), z, local_weight, bias, rb_bias, rb, cols, spectral_weight, devices
    )
    grad_input, grad_spectral, grad_local, grad_bias = final(
        part, z, rb, cols, own_modes, delta_modes, small, height
    )
    return (
        grad_input.reshape(inputs.shape),
        grad_spectral.reshape(spectral_weight.shape),
        grad_local,
        grad_bias.reshape(chans),
    )


def solution(mesh):
    return jax.shard_map(
        per_device,
        mesh=mesh,
        in_specs=(
            P("dom", None, "space", None),
            P("dom", None, "space", None),
            P("space", None, None, None),
            P(),
            P(),
        ),
        out_specs=(
            P("dom", None, "space", None),
            P("space", "dom", None, None),
            P("dom", None),
            P("dom"),
        ),
        check_vma=False,
    )
```
